128 devices in a mesh: row: 16 (over y, z_hi, core), col: 8 (over x, z_lo).
Axes of the slice: x: 4, y: 4, z: 4 (z_hi: 2, z_lo: 2; z = z_hi * 2 + z_lo), core: 2. Of those that a mesh axis runs over, the one named last changes fastest.
Arguments:
- stored: float32 [768, 4, 256, 256], P(('row', 'col'))
- pattern: int32 [768, 4], P(('row', 'col')), may hold values from 0 to 1, as said below
Outputs:
- purified: float32 [768, 4, 256, 256], P(('row', 'col'))
The draws below stay inside these ranges and needn't reach their ends.
Inputs may be any that keep to these rules, and one draw needn't show every extreme that they name: pattern[i, 0] is 1 for every i, and pattern[i, d] is 0 wherever i + d >= 768.
All inputs are finite; a program needn't handle non-finite values.
Results may differ from the reference program's by a relative error of at most 0.0003.
Values sent between devices are 32-bit elements; how exact they have to be, the bound alone decides.
No kernel may reach another device: no remote copies, remote signals or barrier semaphores. Data moves between devices by JAX's collectives and lax.ppermute only.
A program may use at most 256 MiB of HBM per device.

```python
import jax
import jax.numpy as jnp
from jax import lax

BS = 256
W = 3
STEPS = 2
NB = 768
NOCC = 78643


def draw_stored(key, part):
    key = jax.random.fold_in(key, 11)
    noise_key, level_key = jax.random.split(key)
    shape = (NB, W + 1, BS, BS)
    noise = jax.random.normal(noise_key, shape, jnp.float32) * 0.01
    level = jax.random.uniform(level_key, (NB, BS), jnp.float32, 0.3, 0.7)
    identity = jnp.eye(BS, dtype=jnp.float32)
    diagonal_part = noise[:, 0] + level[:, :, None] * identity
    return noise.at[:, 0].set(diagonal_part)


def draw_pattern(key, part):
    key = jax.random.fold_in(key, 5)
    picked = jax.random.randint(key, (NB, W + 1), 0, 2)
    row_ids = jnp.arange(NB, dtype=jnp.int32)[:, None]
    offsets = jnp.arange(W + 1, dtype=jnp.int32)[None, :]
    picked = jnp.where(offsets == 0, 1, picked)
    return jnp.where(row_ids + offsets < NB, picked, 0).astype(jnp.int32)


def setup_inputs(seed: int = 0) -> dict:
    arg_keys = jax.random.split(jax.random.key(seed), 3)
    return {
        "stored": draw_stored(jax.random.fold_in(arg_keys[2], 71), 0),
        "pattern": draw_pattern(jax.random.fold_in(arg_keys[2], 71), 0),
    }


def block_at(padded, first_row, offset, rows_out):
    if offset >= 0:
        return lax.slice_in_dim(padded, first_row, first_row + rows_out, axis=0)[:, offset], False
    picked = lax.slice_in_dim(padded, first_row + offset, first_row + offset + rows_out, axis=0)[:, -offset]
    return picked, True


def band_square(padded):
    rows_out = padded.shape[0] - 2 * W
    columns = []
    for offset in range(W + 1):
        total = jnp.zeros((rows_out,) + padded.shape[2:], jnp.float32)
        for inner in range(offset - W, W + 1):
            left_block, left_flip = block_at(padded, W, inner, rows_out)
            right_block, right_flip = block_at(padded, W + inner, offset - inner, rows_out)
            form = ("rji" if left_flip else "rij") + "," + ("rkj" if right_flip else "rjk") + "->rik"
            total = total + jnp.einsum(form, left_block, right_block, precision=lax.Precision.HIGHEST)
        columns.append(total)
    return jnp.stack(columns, axis=1)


def reference(stored, pattern):
    support = pattern.astype(jnp.float32)[:, :, None, None]
    diagonal_part = stored[:, 0]
    symmetric = 0.5 * (diagonal_part + jnp.swapaxes(diagonal_part, 1, 2))
    current = stored.at[:, 0].set(symmetric) * support
    target = jnp.float32(NOCC)
    for sweep in range(STEPS):
        trace_one = jnp.sum(jnp.diagonal(current[:, 0], axis1=1, axis2=2))
        trace_two = jnp.sum(current[:, 0] * current[:, 0]) + 2.0 * jnp.sum(current[:, 1:] * current[:, 1:])
        padded = jnp.pad(current, ((W, W), (0, 0), (0, 0), (0, 0)))
        product = band_square(padded) * support
        mixing = (target - trace_two) / (2.0 * (trace_one - trace_two))
        current = (1.0 - 2.0 * mixing) * product + 2.0 * mixing * current
    return current
```

```python
import functools

import jax
import jax.numpy as jnp
from jax import lax
from jax.experimental import pallas as pl
from jax.experimental.pallas import tpu as pltpu
from jax.sharding import PartitionSpec as P

W = 3
BS = 256
HALF = 128
AXES = ("row", "col")
UPPER = ((0, 0), (0, 1), (0, 2), (1, 1), (1, 2), (2, 2))
LOWER = ((0, 0), (1, 0), (1, 1), (2, 0), (2, 1), (2, 2))
OFFDIAG = ((0, 1), (0, 2), (1, 2))
PACKED = 3 * 512 + 3 * 256 + 8
F32 = jnp.float32
BF16 = jnp.bfloat16
VMEM_LIMIT = 48 * 2**20
PASS_FLOPS = 2 * BS**3 * 3


def at_b(r, c):
    return r, c - r


def at_a(r, c):
    return 3 + r, c - r


def at_d(r, c):
    return r, 3 + c - r


def at_c(r, c):
    return 3 + r, 3 + c - r


def split(x):
    hi = x.astype(BF16)
    return hi, (x - hi.astype(F32)).astype(BF16)


def grid2(n):
    return lax.broadcasted_iota(jnp.int32, (n, n), 0), lax.broadcasted_iota(jnp.int32, (n, n), 1)


def symmetric(x):
    return 0.5 * (x + x.T)


def present(pattern, rd):
    return pattern[rd[0], rd[1]].astype(F32)


def pack(msg, blocks, flags):
    for n, rc in enumerate(OFFDIAG):
        x = blocks(rc)
        msg[512 * n : 512 * n + 256, :] = x[:, :HALF]
        msg[512 * n + 256 : 512 * n + 512, :] = x[:, HALF:]
    rows, cols = grid2(HALF)
    tail = []
    for r in range(3):
        x = blocks((r, r))
        base = 1536 + 256 * r
        first, second = x[:HALF, :HALF], x[HALF:, HALF:]
        msg[base : base + HALF, :] = x[:HALF, HALF:]
        msg[base + HALF : base + 256, :] = jnp.where(rows <= cols, first, second)
        tail.append(jnp.sum(jnp.where(rows == cols, second, 0.0), axis=0, keepdims=True))
    for f in flags:
        tail.append(jnp.full((1, HALF), f, F32))
    tail.append(jnp.zeros((8 - len(tail), HALF), F32))
    msg[2304:2312, :] = jnp.concatenate(tail, axis=0)


def unpack_off(msg, n):
    return jnp.concatenate([msg[512 * n : 512 * n + 256, :], msg[512 * n + 256 : 512 * n + 512, :]], axis=1)


def unpack_diag(msg, r):
    rows, cols = grid2(HALF)
    base = 1536 + 256 * r
    corner = msg[base : base + HALF, :]
    both = msg[base + HALF : base + 256, :]
    flipped = both.T
    line = msg[2304 + r : 2305 + r, :]
    first = jnp.where(rows <= cols, both, flipped)
    second = jnp.where(rows > cols, both, flipped)
    second = jnp.where(rows == cols, line, second)
    return jnp.concatenate(
        [jnp.concatenate([first, corner], axis=1), jnp.concatenate([corner.T, second], axis=1)], axis=0
    )


def unpack(msg, rc):
    return unpack_diag(msg, rc[0]) if rc[0] == rc[1] else unpack_off(msg, OFFDIAG.index(rc))


def flag_of(msg, rc):
    n = OFFDIAG.index(rc)
    return msg[2307 + n : 2308 + n, 0:1]


class Split:
    def __init__(self, hi, lo, r0=0, c0=0):
        self.hi, self.lo, self.r0, self.c0 = hi, lo, r0, c0

    def at(self, r, c0, c1):
        r, c0, c1 = r - self.r0, c0 - self.c0, c1 - self.c0
        return (slice(BS * r, BS * (r + 1)), slice(BS * c0, BS * c1))

    def put(self, r, c, x):
        hi, lo = split(x)
        where = self.at(r, c, c + 1)
        self.hi[where] = hi
        self.lo[where] = lo

    def put_both(self, r, c, x):
        self.put(r, c, x)
        if r != c:
            self.put(c, r, x.T)


def times(left, i, right, j, k0, k1):
    def dot(x, y):
        return lax.dot_general(x, y, (((1,), (1,)), ((), ())), preferred_element_type=F32)

    wi, wj = left.at(i, k0, k1), right.at(j, k0, k1)
    lh, ll, rh, rl = left.hi[wi], left.lo[wi], right.hi[wj], right.lo[wj]
    return dot(lh, rh) + (dot(lh, rl) + dot(ll, rh))


def fetch(stored, places, buffer, sems):
    copies = [
        pltpu.make_async_copy(stored.at[r, d], buffer.at[n], sems.at[n]) for n, (r, d) in enumerate(places)
    ]
    for copy in copies:
        copy.start()
    seen = set()

    def get(place):
        n = places.index(place)
        if n not in seen:
            copies[n].wait()
            seen.add(n)
        return buffer[n]

    return get


def masked(get, pattern, place):
    x = get(place)
    return symmetric(x) if place[1] == 0 else x * present(pattern, place)


def squares(x):
    y = jnp.sum((x * x).reshape(32, 8, BS), axis=0)
    return y[:, :HALF] + y[:, HALF:]


def diagonals(x):
    rows, cols = grid2(BS)
    y = jnp.sum(jnp.where(rows == cols, x, 0.0).reshape(32, 8, BS), axis=0)
    return y[:, :HALF] + y[:, HALF:]


def outer(hi, lo, groups, blocks):
    t = Split(hi, lo)
    for rc in groups:
        t.put(rc[1], rc[0], blocks(rc).T)
    return t


def gram(t):
    return {rc: times(t, rc[0], t, rc[1], rc[1], 3) for rc in UPPER}


def pack_b(stored, pattern, msg, buffer, sems):
    get = fetch(stored, [at_b(*rc) for rc in UPPER], buffer, sems)
    pack(msg, lambda rc: masked(get, pattern, at_b(*rc)), [present(pattern, at_b(*rc)) for rc in OFFDIAG])


ALL_PLACES = (
    [at_c(*rc) for rc in LOWER] + [at_a(*rc) for rc in UPPER] + [at_d(*rc) for rc in LOWER] + [at_b(*rc) for rc in UPPER]
)


def gram_and_traces(stored, pattern, msg, traces, buffer, hi, lo, sems):
    get = fetch(stored, ALL_PLACES, buffer, sems)
    t = outer(hi, lo, LOWER, lambda rc: masked(get, pattern, at_c(*rc)))
    g = gram(t)
    pack(msg, lambda rc: g[rc], [])
    one = jnp.zeros((8, HALF), F32)
    two = jnp.zeros((8, HALF), F32)
    for place in ALL_PLACES:
        x = masked(get, pattern, place)
        if place[1] == 0:
            one = one + diagonals(x)
            two = two + squares(x)
        else:
            two = two + 2.0 * squares(x)
    traces[0:8, :] = one
    traces[8:16, :] = two


T_PLACES = [at_b(*rc) for rc in UPPER] + [at_d(*rc) for rc in LOWER] + [at_a(*rc) for rc in UPPER]


def square_t(z, pb, pd, keep_e, pattern):
    for n, (r, c) in enumerate(UPPER):
        e = times(z, r, z, c, 3, 3 + min(r, c) + 1)
        if keep_e is not None:
            keep_e[(r, c)] = e
        pb[n] = times(z, r, z, c, 0, 3) + e
    for n, (r, c) in enumerate(LOWER):
        pd[n] = times(z, r, z, 3 + c, c, 3 + r + 1)


def square_s(z, pa, pc):
    for n, (r, c) in enumerate(UPPER):
        pa[n] = times(z, 3 + r, z, 3 + c, c, 6 + r + 1)
    for n, (r, c) in enumerate(LOWER):
        pc[n] = times(z, 3 + r, z, 6 + c, 3 + c, 6)


def fill_t(z, b, d, a):
    for rc in UPPER:
        z.put_both(rc[0], rc[1], b(rc))
    for rc in LOWER:
        z.put_both(rc[0], 3 + rc[1], d(rc))
    for rc in UPPER:
        z.put_both(3 + rc[0], 3 + rc[1], a(rc))


def fill_s(z, d, a, c):
    for rc in LOWER:
        z.put(3 + rc[1], rc[0], d(rc).T)
    for rc in UPPER:
        z.put_both(3 + rc[0], 3 + rc[1], a(rc))
    for rc in LOWER:
        z.put_both(3 + rc[0], 6 + rc[1], c(rc))


def first_t(stored, pattern, pb, pd, msg, buffer, hi, lo, sems):
    get = fetch(stored, T_PLACES, buffer, sems)
    z = Split(hi, lo)
    fill_t(
        z,
        lambda rc: masked(get, pattern, at_b(*rc)),
        lambda rc: masked(get, pattern, at_d(*rc)),
        lambda rc: masked(get, pattern, at_a(*rc)),
    )
    e = {}
    square_t(z, pb, pd, e, pattern)
    pack(msg, lambda rc: e[rc], [])


S_PLACES = [at_d(*rc) for rc in LOWER] + [at_a(*rc) for rc in UPPER] + [at_c(*rc) for rc in LOWER]


def first_s(stored, pattern, pa, pc, buffer, hi, lo, sems):
    get = fetch(stored, S_PLACES, buffer, sems)
    z = Split(hi, lo, 3, 0)
    fill_s(
        z,
        lambda rc: masked(get, pattern, at_d(*rc)),
        lambda rc: masked(get, pattern, at_a(*rc)),
        lambda rc: masked(get, pattern, at_c(*rc)),
    )
    square_s(z, pa, pc)


def next_c(stored, msg_b, pc, pattern, mix, c1, msg_g, buffer, chi, clo, bhi, blo, thi, tlo, sems):
    get = fetch(stored, [at_c(*rc) for rc in LOWER], buffer, sems)
    cs, bs = Split(chi, clo), Split(bhi, blo)
    for rc in UPPER:
        bs.put_both(rc[0], rc[1], unpack(msg_b, rc))
    for rc in LOWER:
        cs.put(rc[0], rc[1], masked(get, pattern, at_c(*rc)))
    a, b = mix[0], mix[1]
    t = Split(thi, tlo)
    for n, (r, c) in enumerate(LOWER):
        place = at_c(r, c)
        keep = present(pattern, place)
        x = (a * keep) * (pc[n] + times(cs, r, bs, c, 0, r + 1)) + (b * keep) * get(place)
        c1[n] = x
        t.put(c, r, x.T)
    g = gram(t)
    pack(msg_g, lambda rc: g[rc], [])


def next_b(stored, msg_g, pb, pattern, mix, b1, traces, buffer, sems):
    get = fetch(stored, [at_b(*rc) for rc in UPPER], buffer, sems)
    a, b = mix[0], mix[1]
    one = jnp.zeros((8, HALF), F32)
    two = jnp.zeros((8, HALF), F32)
    for n, rc in enumerate(UPPER):
        place = at_b(*rc)
        p = pb[n] + unpack(msg_g, rc)
        x = masked(get, pattern, place)
        if place[1] == 0:
            x = a * p + b * x
            one = one + diagonals(x)
            two = two + squares(x)
        else:
            x = (a * present(pattern, place)) * p + b * x
            two = two + 2.0 * squares(x)
        b1[n] = x
    traces[0:8, :] = one
    traces[8:16, :] = two


def second_s(stored, pa, pd, c1, pattern, mix, a1, d1, pa1, pc1, traces, buffer, hi, lo, sems):
    places = [at_d(*rc) for rc in LOWER] + [at_a(*rc) for rc in UPPER]
    get = fetch(stored, places, buffer, sems)
    a, b = mix[0], mix[1]
    one = jnp.zeros((8, HALF), F32)
    two = jnp.zeros((8, HALF), F32)
    for n, rc in enumerate(LOWER):
        keep = present(pattern, at_d(*rc))
        d1[n] = (a * keep) * pd[n] + (b * keep) * get(at_d(*rc))
        two = two + 2.0 * squares(d1[n])
        two = two + 2.0 * squares(c1[n])
    for n, rc in enumerate(UPPER):
        place = at_a(*rc)
        x = masked(get, pattern, place)
        if place[1] == 0:
            x = a * pa[n] + b * x
            one = one + diagonals(x)
            two = two + squares(x)
        else:
            x = (a * present(pattern, place)) * pa[n] + b * x
            two = two + 2.0 * squares(x)
        a1[n] = x
    traces[0:8, :] = one
    traces[8:16, :] = two
    z = Split(hi, lo, 3, 0)
    fill_s(
        z,
        lambda rc: d1[LOWER.index(rc)],
        lambda rc: a1[UPPER.index(rc)],
        lambda rc: c1[LOWER.index(rc)],
    )
    square_s(z, pa1, pc1)


def second_t(b1, d1, a1, pb1, pd1, hi, lo):
    z = Split(hi, lo)
    fill_t(
        z,
        lambda rc: b1[UPPER.index(rc)],
        lambda rc: d1[LOWER.index(rc)],
        lambda rc: a1[UPPER.index(rc)],
    )
    square_t(z, pb1, pd1, None, None)


def across(msg_b, msg_e, msg_g, c1, pc1, mix, out, bhi, blo, chi, clo, nhi, nlo):
    a, b = mix[0], mix[1]
    bs, cs, ns = Split(bhi, blo), Split(chi, clo), Split(nhi, nlo)
    for rc in UPPER:
        bs.put_both(rc[0], rc[1], unpack(msg_b, rc))
    for n, rc in enumerate(LOWER):
        cs.put(rc[0], rc[1], c1[n])
    for rc in UPPER:
        r, c = rc
        p = times(bs, r, bs, c, 0, 3) + (unpack(msg_e, rc) + unpack(msg_g, rc))
        if r != c:
            p = p * flag_of(msg_b, rc)
        ns.put_both(r, c, a * p + b * unpack(msg_b, rc))
    for n, (r, c) in enumerate(LOWER):
        out[n] = pc1[n] + times(cs, r, ns, c, 0, r + 1)


def finish_most(pa1, pc1, pd1, a1, c1, d1, pattern, mix, out, buffer, sems):
    a, b = mix[0], mix[1]
    copies = []
    groups = ((pd1, d1, LOWER, at_d), (pa1, a1, UPPER, at_a), (pc1, c1, LOWER, at_c))
    for p, x, order, at in groups:
        for n, rc in enumerate(order):
            place = at(*rc)
            k = len(copies)
            scale = a if place[1] == 0 else a * present(pattern, place)
            buffer[k] = scale * p[n] + b * x[n]
            copies.append(pltpu.make_async_copy(buffer.at[k], out.at[place[0], place[1]], sems.at[k]))
            copies[-1].start()
    for copy in copies:
        copy.wait()


def finish_b(base, msg_g, pb1, b1, pattern, mix, out, buffer, sems):
    del base
    a, b = mix[0], mix[1]
    copies = []
    for n, rc in enumerate(UPPER):
        place = at_b(*rc)
        scale = a if place[1] == 0 else a * present(pattern, place)
        buffer[n] = scale * (pb1[n] + unpack(msg_g, rc)) + b * b1[n]
        copies.append(pltpu.make_async_copy(buffer.at[n], out.at[place[0], place[1]], sems.at[n]))
        copies[-1].start()
    for copy in copies:
        copy.wait()


HBM = pl.BlockSpec(memory_space=pl.ANY)
VMEM = pl.BlockSpec(memory_space=pltpu.VMEM)
SMEM = pl.BlockSpec(memory_space=pltpu.SMEM)
MSG = jax.ShapeDtypeStruct((PACKED, HALF), F32)
SIX = jax.ShapeDtypeStruct((6, BS, BS), F32)
TRACES = jax.ShapeDtypeStruct((16, HALF), F32)


def blocks_buffer(n):
    return pltpu.VMEM((n, BS, BS), F32)


def parts(rows, cols):
    return [pltpu.VMEM((BS * rows, BS * cols), BF16)] * 2


def call(body, name, ins, in_specs, outs, out_specs, scratch, products, moved, aliases=None):
    return pl.pallas_call(
        body,
        out_shape=outs,
        in_specs=in_specs,
        out_specs=out_specs,
        scratch_shapes=scratch,
        input_output_aliases=aliases or {},
        cost_estimate=pl.CostEstimate(flops=products * PASS_FLOPS, bytes_accessed=moved * 4 * BS * BS, transcendentals=0),
        compiler_params=pltpu.CompilerParams(vmem_limit_bytes=VMEM_LIMIT),
        name=name,
    )(*ins)


def shift(x, step):
    count = lax.axis_size(AXES)
    pairs = [(i, i + step) for i in range(count) if 0 <= i + step < count]
    return lax.ppermute(x, AXES, pairs)


def total(x):
    count = lax.axis_size(AXES)
    bit = 1
    while bit < count:
        width = min(4, count // bit)
        got = [
            lax.ppermute(x, AXES, [(i, i ^ (bit * k)) for i in range(count)]) for k in range(1, width)
        ]
        for y in got:
            x = x + y
        bit *= width
    return x


def weights(traces, target):
    one = jnp.sum(traces[0:8])
    two = jnp.sum(traces[8:16])
    mixing = (target - two) / (2.0 * (one - two))
    return jnp.stack([1.0 - 2.0 * mixing, 2.0 * mixing])


def local(stored, pattern):
    target = jnp.float32(stored.shape[0] * lax.axis_size(AXES) * stored.shape[2] * 2 // 5)
    dma = pltpu.SemaphoreType.DMA

    msg_b = call(
        pack_b, "pack_b", (stored, pattern), [HBM, SMEM], MSG, VMEM, [blocks_buffer(6), dma((6,))], 0, 11
    )
    next_block = shift(msg_b, -1)

    msg_g, traces = call(
        gram_and_traces, "gram_and_traces", (stored, pattern), [HBM, SMEM], (MSG, TRACES), (VMEM, VMEM),
        [blocks_buffer(24)] + parts(3, 3) + [dma((24,))], 10, 30,
    )
    from_prev = shift(msg_g, 1)
    mix1 = weights(total(traces), target)

    pb, pd, msg_e = call(
        first_t, "first_t", (stored, pattern), [HBM, SMEM], (SIX, SIX, MSG), (VMEM, VMEM, VMEM),
        [blocks_buffer(18)] + parts(6, 6) + [dma((18,))], 56, 36,
    )
    pa, pc = call(
        first_s, "first_s", (stored, pattern), [HBM, SMEM], (SIX, SIX), (VMEM, VMEM),
        [blocks_buffer(18)] + parts(6, 9) + [dma((18,))], 52, 30,
    )
    msg_e, mix1 = lax.optimization_barrier((msg_e, mix1))
    next_e = shift(msg_e, -1)

    c1, msg_g1 = call(
        next_c, "next_c", (stored, next_block, pc, pattern, mix1), [HBM, VMEM, VMEM, SMEM, SMEM], (SIX, MSG),
        (VMEM, VMEM), [blocks_buffer(6)] + parts(3, 3) + parts(3, 3) + parts(3, 3) + [dma((6,))], 24, 30,
    )
    from_prev1 = shift(msg_g1, 1)

    a1, d1, pa1, pc1, traces_s = call(
        second_s, "second_s", (stored, pa, pd, c1, pattern, mix1), [HBM, VMEM, VMEM, VMEM, SMEM, SMEM],
        (SIX, SIX, SIX, SIX, TRACES), (VMEM,) * 5, [blocks_buffer(12)] + parts(6, 9) + [dma((12,))], 52, 60,
    )
    b1, traces_t = call(
        next_b, "next_b", (stored, from_prev, pb, pattern, mix1), [HBM, VMEM, VMEM, SMEM, SMEM], (SIX, TRACES),
        (VMEM, VMEM), [blocks_buffer(6), dma((6,))], 0, 25,
    )
    mix2 = weights(total(traces_s + traces_t), target)
    pb1, pd1 = call(
        second_t, "second_t", (b1, d1, a1), [VMEM, VMEM, VMEM], (SIX, SIX), (VMEM, VMEM), parts(6, 6), 56, 30
    )
    pc1 = call(
        across, "across", (next_block, next_e, msg_g, c1, pc1, mix1), [VMEM] * 5 + [SMEM], SIX, VMEM,
        parts(3, 3) + parts(3, 3) + parts(3, 3), 32, 35,
    )
    out = jax.ShapeDtypeStruct(stored.shape, F32)
    most = call(
        finish_most, "finish_most", (pa1, pc1, pd1, a1, c1, d1, pattern, mix2), [VMEM] * 6 + [SMEM, SMEM], out, HBM,
        [blocks_buffer(18), dma((18,))], 0, 54,
    )
    return call(
        finish_b, "finish_b", (most, from_prev1, pb1, b1, pattern, mix2), [HBM, VMEM, VMEM, VMEM, SMEM, SMEM], out, HBM,
        [blocks_buffer(6), dma((6,))], 0, 24, {0: 0},
    )


def solution(mesh):
    in_specs = (P(AXES, None, None, None), P(AXES, None))
    out_specs = P(AXES, None, None, None)
    return jax.shard_map(local, mesh=mesh, in_specs=in_specs, out_specs=out_specs, check_vma=False)
```

```python
import functools

import jax
import jax.numpy as jnp
from jax import lax
from jax.experimental import pallas as pl
from jax.experimental.pallas import tpu as pltpu
from jax.sharding import PartitionSpec as P

BS = 256
HALF = 128
AXES = ("row", "col")
UPPER = ((0, 0), (0, 1), (0, 2), (1, 1), (1, 2), (2, 2))
LOWER = ((0, 0), (1, 0), (1, 1), (2, 0), (2, 1), (2, 2))
OFFDIAG = ((0, 1), (0, 2), (1, 2))
PACKED = 3 * 512 + 3 * 256 + 8
F32 = jnp.float32
BF16 = jnp.bfloat16


def at_b(r, c):
    return r, c - r


def at_a(r, c):
    return 3 + r, c - r


def at_d(r, c):
    return r, 3 + c - r


def at_c(r, c):
    return 3 + r, 3 + c - r


def weights(traces, target):
    def all_of(x):
        return jnp.sum(jnp.sum(x, axis=0, keepdims=True), axis=1, keepdims=True)

    one, two = all_of(traces[0:8, :]), all_of(traces[8:16, :])
    mixing = (target - two) / (2.0 * (one - two))
    return 1.0 - 2.0 * mixing, 2.0 * mixing


def flag(flags, place):
    return flags[place[0] : place[0] + 1, place[1] : place[1] + 1]


def split(x):
    hi = x.astype(BF16)
    return hi, (x - hi.astype(F32)).astype(BF16)


def grid2(n):
    return lax.broadcasted_iota(jnp.int32, (n, n), 0), lax.broadcasted_iota(jnp.int32, (n, n), 1)


def symmetric(x):
    return 0.5 * (x + x.T)


def present(pattern, rd):
    return pattern[rd[0], rd[1]].astype(F32)


def pack(msg, blocks, flags):
    for n, rc in enumerate(OFFDIAG):
        x = blocks(rc)
        msg[512 * n : 512 * n + 256, :] = x[:, :HALF]
        msg[512 * n + 256 : 512 * n + 512, :] = x[:, HALF:]
    rows, cols = grid2(HALF)
    tail = []
    for r in range(3):
        x = blocks((r, r))
        base = 1536 + 256 * r
        first, second = x[:HALF, :HALF], x[HALF:, HALF:]
        msg[base : base + HALF, :] = x[:HALF, HALF:]
        msg[base + HALF : base + 256, :] = jnp.where(rows <= cols, first, second)
        tail.append(jnp.sum(jnp.where(rows == cols, second, 0.0), axis=0, keepdims=True))
    for f in flags:
        tail.append(jnp.full((1, HALF), f, F32))
    tail.append(jnp.zeros((8 - len(tail), HALF), F32))
    msg[2304:2312, :] = jnp.concatenate(tail, axis=0)


def unpack_off(msg, n):
    return jnp.concatenate([msg[512 * n : 512 * n + 256, :], msg[512 * n + 256 : 512 * n + 512, :]], axis=1)


def unpack_diag(msg, r):
    rows, cols = grid2(HALF)
    base = 1536 + 256 * r
    corner = msg[base : base + HALF, :]
    both = msg[base + HALF : base + 256, :]
    flipped = both.T
    line = msg[2304 + r : 2305 + r, :]
    first = jnp.where(rows <= cols, both, flipped)
    second = jnp.where(rows > cols, both, flipped)
    second = jnp.where(rows == cols, line, second)
    return jnp.concatenate(
        [jnp.concatenate([first, corner], axis=1), jnp.concatenate([corner.T, second], axis=1)], axis=0
    )


def unpack(msg, rc):
    return unpack_diag(msg, rc[0]) if rc[0] == rc[1] else unpack_off(msg, OFFDIAG.index(rc))


def flag_of(msg, rc):
    n = OFFDIAG.index(rc)
    return msg[2307 + n : 2308 + n, 0:1]


def upper(hl, r, c):
    hi, lo = hl
    if r <= c:
        n = UPPER.index((r, c))
        return hi[n], lo[n], False
    n = UPPER.index((c, r))
    return hi[n], lo[n], True


def lower(hl, r, c):
    n = LOWER.index((r, c))
    return hl[0][n], hl[1][n], False


def flipped(x):
    return x[0], x[1], not x[2]


def multiply(x, y):
    dims = (((0 if x[2] else 1,), (1 if y[2] else 0,)), ((), ()))

    def dot(p, q):
        return lax.dot_general(p, q, dims, preferred_element_type=F32)

    return dot(x[0], y[0]) + (dot(x[0], y[1]) + dot(x[1], y[0]))


def add_up(pairs):
    total = None
    for x, y in pairs:
        product = multiply(x, y)
        total = product if total is None else total + product
    return total


def gram(c):
    return {
        (r, s): add_up((flipped(lower(c, k, r)), lower(c, k, s)) for k in range(s, 3)) for r, s in UPPER
    }


def fetch(stored, places, buffer, sems):
    copies = [
        pltpu.make_async_copy(stored.at[r, d], buffer.at[n], sems.at[n]) for n, (r, d) in enumerate(places)
    ]
    for copy in copies:
        copy.start()
    return copies


def squares(x):
    y = jnp.sum((x * x).reshape(32, 8, BS), axis=0)
    return y[:, :HALF] + y[:, HALF:]


def diagonals(x):
    rows, cols = grid2(BS)
    y = jnp.sum(jnp.where(rows == cols, x, 0.0).reshape(32, 8, BS), axis=0)
    return y[:, :HALF] + y[:, HALF:]


class Traces:
    def __init__(self):
        self.one = jnp.zeros((8, HALF), F32)
        self.two = jnp.zeros((8, HALF), F32)

    def add(self, x, place):
        if place[1] == 0:
            self.one = self.one + diagonals(x)
            self.two = self.two + squares(x)
        else:
            self.two = self.two + 2.0 * squares(x)

    def write(self, ref):
        ref[0:8, :] = self.one
        ref[8:16, :] = self.two


def pack_b(stored, whole_pattern, msg, buffer, pattern, sems, pattern_sem):
    copies = fetch(stored, [at_b(*rc) for rc in UPPER], buffer, sems)
    flags = pltpu.make_async_copy(whole_pattern, pattern, pattern_sem)
    flags.start()
    flags.wait()

    def block(rc):
        n = UPPER.index(rc)
        copies[n].wait()
        x = buffer[n]
        return symmetric(x) if rc[0] == rc[1] else x * present(pattern, at_b(*rc))

    pack(msg, block, [present(pattern, at_b(*rc)) for rc in OFFDIAG])


GROUPS = (("c", LOWER, at_c), ("a", UPPER, at_a), ("d", LOWER, at_d), ("b", UPPER, at_b))
PLACES = [at(*rc) for _, order, at in GROUPS for rc in order]


def prepare(
    stored, whole_pattern, dep, xc, xa, xd, xb, ch, cl, ah, al, dh, dl, bh, bl, msg, traces, flags, buffer, pattern,
    sems, pattern_sem,
):
    del dep
    copies = fetch(stored, PLACES, buffer, sems)
    copy = pltpu.make_async_copy(whole_pattern, pattern, pattern_sem)
    copy.start()
    copy.wait()
    rows, cols = (lax.broadcasted_iota(jnp.int32, (8, HALF), n) for n in (0, 1))
    table = jnp.zeros((8, HALF), F32)
    for place in PLACES:
        table = jnp.where((rows == place[0]) & (cols == place[1]), present(pattern, place), table)
    flags[...] = table
    t = Traces()
    for g, (x_ref, hi, lo) in enumerate(((xc, ch, cl), (xa, ah, al), (xd, dh, dl), (xb, bh, bl))):
        for n in range(6):
            k = 6 * g + n
            place = PLACES[k]
            copies[k].wait()
            x = buffer[k]
            x = symmetric(x) if place[1] == 0 else x * present(pattern, place)
            x_ref[n] = x
            hi[n], lo[n] = split(x)
            t.add(x, place)
        if g == 0:
            products = gram((ch, cl))
            pack(msg, lambda rc: products[rc], [])
    t.write(traces)


def product_c(ah, al, ch, cl, dep, pc):
    del dep
    a, c = (ah, al), (ch, cl)
    for n, (r, s) in enumerate(LOWER):
        pc[n] = add_up((upper(a, r, k), lower(c, k, s)) for k in range(s, 3))


def product_a(ah, al, ch, cl, dh, dl, dep, pa):
    del dep
    a, c, d = (ah, al), (ch, cl), (dh, dl)
    for n, (r, s) in enumerate(UPPER):
        pairs = [(flipped(lower(d, k, r)), lower(d, k, s)) for k in range(s, 3)]
        pairs += [(upper(a, r, k), upper(a, k, s)) for k in range(3)]
        pairs += [(lower(c, r, k), flipped(lower(c, s, k))) for k in range(r + 1)]
        pa[n] = add_up(pairs)


def own_b(b, d, r, s):
    pairs = [(upper(b, r, k), upper(b, k, s)) for k in range(3)]
    pairs += [(lower(d, r, k), flipped(lower(d, s, k))) for k in range(r + 1)]
    return add_up(pairs)


def product_b(bh, bl, dh, dl, dep, pb):
    del dep
    for n, (r, s) in enumerate(UPPER):
        pb[n] = own_b((bh, bl), (dh, dl), r, s)


def product_b_packed(bh, bl, dh, dl, dep, pb, msg):
    del dep
    for n, (r, s) in enumerate(UPPER):
        pb[n] = own_b((bh, bl), (dh, dl), r, s)
    pack(msg, lambda rc: pb[UPPER.index(rc)], [])


def product_d(bh, bl, dh, dl, ah, al, dep, pd):
    del dep
    a, b, d = (ah, al), (bh, bl), (dh, dl)
    for n, (r, s) in enumerate(LOWER):
        pairs = [(upper(b, r, k), lower(d, k, s)) for k in range(s, 3)]
        pairs += [(lower(d, r, k), upper(a, k, s)) for k in range(r + 1)]
        pd[n] = add_up(pairs)


def next_c(target, msg_b, xc, ch, cl, pc, flags, traces, c1, c1h, c1l, msg_g, bh, bl):
    for n, rc in enumerate(UPPER):
        bh[n], bl[n] = split(unpack(msg_b, rc))
    a, b = weights(traces, target)
    old, nb = (ch, cl), (bh, bl)
    for n, (r, s) in enumerate(LOWER):
        p = pc[n] + add_up((lower(old, r, k), upper(nb, k, s)) for k in range(r + 1))
        x = (a * flag(flags, at_c(r, s))) * p + b * xc[n]
        c1[n] = x
        c1h[n], c1l[n] = split(x)
    products = gram((c1h, c1l))
    pack(msg_g, lambda rc: products[rc], [])


def next_rest(
    target, msg_g, xb, xd, xa, pb, pd, pa, c1, flags, old_traces, b1, d1, a1, b1h, b1l, d1h, d1l, a1h, a1l, traces
):
    a, b = weights(old_traces, target)
    t = Traces()
    work = (
        (xa, pa, a1, a1h, a1l, UPPER, at_a),
        (xd, pd, d1, d1h, d1l, LOWER, at_d),
        (xb, pb, b1, b1h, b1l, UPPER, at_b),
    )
    for old, product, new, hi, lo, order, at in work:
        for n, rc in enumerate(order):
            place = at(*rc)
            p = product[n]
            if at is at_b:
                p = p + unpack(msg_g, rc)
            scale = a if place[1] == 0 else a * flag(flags, place)
            x = scale * p + b * old[n]
            new[n] = x
            hi[n], lo[n] = split(x)
            t.add(x, place)
    for n, rc in enumerate(LOWER):
        t.add(c1[n], at_c(*rc))
    t.write(traces)


def across(target, msg_b, msg_e, msg_g, c1h, c1l, pc1, traces, dep, out, nh, nl):
    del dep
    a, b = weights(traces, target)
    for n, rc in enumerate(UPPER):
        p = unpack(msg_e, rc) + unpack(msg_g, rc)
        if rc[0] != rc[1]:
            p = p * flag_of(msg_b, rc)
        nh[n], nl[n] = split(a * p + b * unpack(msg_b, rc))
    c, nb = (c1h, c1l), (nh, nl)
    for n, (r, s) in enumerate(LOWER):
        out[n] = pc1[n] + add_up((lower(c, r, k), upper(nb, k, s)) for k in range(r + 1))


def finish_most(target, pa1, pc1, pd1, a1, c1, d1, flags, traces, out, buffer, sems):
    a, b = weights(traces, target)
    copies = []
    groups = ((pd1, d1, LOWER, at_d), (pa1, a1, UPPER, at_a), (pc1, c1, LOWER, at_c))
    for p, x, order, at in groups:
        for n, rc in enumerate(order):
            place = at(*rc)
            k = len(copies)
            scale = a if place[1] == 0 else a * flag(flags, place)
            buffer[k] = scale * p[n] + b * x[n]
            copies.append(pltpu.make_async_copy(buffer.at[k], out.at[place[0], place[1]], sems.at[k]))
            copies[-1].start()
    for copy in copies:
        copy.wait()


def finish_b(target, base, msg_g, pb1, b1, flags, traces, out, buffer, sems):
    del base
    a, b = weights(traces, target)
    copies = []
    for n, rc in enumerate(UPPER):
        place = at_b(*rc)
        scale = a if place[1] == 0 else a * flag(flags, place)
        buffer[n] = scale * (pb1[n] + unpack(msg_g, rc)) + b * b1[n]
        copies.append(pltpu.make_async_copy(buffer.at[n], out.at[place[0], place[1]], sems.at[n]))
        copies[-1].start()
    for copy in copies:
        copy.wait()


HBM = pl.BlockSpec(memory_space=pltpu.HBM)
ANY = pl.BlockSpec(memory_space=pl.ANY)
VMEM = pl.BlockSpec(memory_space=pltpu.VMEM)
MSG = jax.ShapeDtypeStruct((PACKED, HALF), F32)
SIX = jax.ShapeDtypeStruct((6, BS, BS), F32)
SIX16 = jax.ShapeDtypeStruct((6, BS, BS), BF16)
TRACES = jax.ShapeDtypeStruct((16, HALF), F32)
FLAGS = jax.ShapeDtypeStruct((8, HALF), F32)
PATTERN = [pltpu.SMEM((6, 4), jnp.int32)]
DMA = pltpu.SemaphoreType.DMA


def blocks(n, dtype=F32):
    return pltpu.VMEM((n, BS, BS), dtype)


def call(body, limit, ins, outs, scratch=(), specs=None, out_spec=VMEM, aliases=None, target=None):
    many = isinstance(outs, (list, tuple))
    in_specs = [(specs or {}).get(n, VMEM) for n in range(len(ins))]
    return pl.pallas_call(
        body if target is None else functools.partial(body, target),
        out_shape=outs,
        in_specs=in_specs,
        out_specs=[out_spec] * len(outs) if many else out_spec,
        scratch_shapes=list(scratch),
        input_output_aliases=aliases or {},
        cost_estimate=pl.CostEstimate(flops=1024, bytes_accessed=1024, transcendentals=0),
        compiler_params=pltpu.CompilerParams(vmem_limit_bytes=limit * 2**20),
        name=getattr(body, "__name__", "add_arrays"),
    )(*ins)


def shift(x, step):
    count = lax.axis_size(AXES)
    pairs = [(i, i + step) for i in range(count) if 0 <= i + step < count]
    return lax.ppermute(x, AXES, pairs)


def place_of(i):
    return i // 2 % 4, i // 32, i // 16 % 2 * 2 + i % 2, i // 8 % 2


def index_of(x, y, z, core):
    return ((y % 4 * 2 + z % 4 // 2) * 2 + core % 2) * 8 + x % 4 * 2 + z % 2


def add_arrays(count, *refs):
    total = refs[0][...]
    for ref in refs[1:count]:
        total = total + ref[...]
    refs[-1][...] = total


def total(x, kernels):
    kernels = list(kernels)
    results = []
    count = lax.axis_size(AXES)

    def moved(v, f):
        return lax.ppermute(v, AXES, [(i, f(i)) for i in range(count)])

    def by(f):
        return lambda i: index_of(*f(*place_of(i)))

    def finished(x, arrived):
        ins = [x, *arrived]
        specs = {}
        if kernels:
            results.append(kernels.pop(0)(x))
            last = results[-1]
            specs[len(ins)] = ANY
            ins.append(last[0] if isinstance(last, (list, tuple)) else last)
        return call(functools.partial(add_arrays, 1 + len(arrived)), 1, ins, TRACES, specs=specs)

    if (lax.axis_size("row"), lax.axis_size("col")) != (16, 8):
        for k in range(count.bit_length() - 1):
            x = finished(x, [moved(x, lambda i: i ^ (1 << k))])
    else:
        passed = x
        for _ in range(3):
            passed = moved(passed, by(lambda x, y, z, c: (x + (1 if z % 2 == 0 else -1), y, z, c)))
            x = finished(x, [passed])
        x = finished(x, [moved(x, by(lambda x, y, z, c: (x, y + k, z + k, c))) for k in (1, 2, 3)])
        x = finished(x, [moved(x, by(lambda x, y, z, c: (x, y + k, z, c))) for k in (1, 2, 3)])
        x = finished(x, [moved(x, by(lambda x, y, z, c: (x, y, z, c + 1)))])
    while kernels:
        results.append(kernels.pop(0)(x))
    return x, results


def local(stored, pattern):
    target = float(stored.shape[0] * lax.axis_size(AXES) * stored.shape[2] * 2 // 5)

    msg_b = call(
        pack_b, 6, (stored, pattern), MSG, [blocks(6), *PATTERN, DMA((6,)), DMA(())], {0: HBM, 1: HBM}
    )
    next_block = shift(msg_b, -1)
    xc, xa, xd, xb, ch, cl, ah, al, dh, dl, bh, bl, msg_g, traces, flags = call(
        prepare, 24, (stored, pattern, msg_b), [SIX] * 4 + [SIX16] * 8 + [MSG, TRACES, FLAGS],
        [blocks(24), *PATTERN, DMA((24,)), DMA(())], {0: HBM, 1: HBM, 2: ANY},
    )
    from_prev = shift(msg_g, 1)

    traces, (pc, pa, (pb, msg_e), pd) = total(
        traces,
        [
            lambda r: call(product_c, 8, (ah, al, ch, cl, r), SIX, specs={4: ANY}),
            lambda r: call(product_a, 8, (ah, al, ch, cl, dh, dl, r), SIX, specs={6: ANY}),
            lambda r: call(product_b_packed, 8, (bh, bl, dh, dl, r), [SIX, MSG], specs={4: ANY}),
            lambda r: call(product_d, 8, (bh, bl, dh, dl, ah, al, r), SIX, specs={6: ANY}),
        ],
    )
    msg_e, traces = lax.optimization_barrier((msg_e, traces))
    next_e = shift(msg_e, -1)

    c1, c1h, c1l, msg_g1 = call(
        next_c, 14, (next_block, xc, ch, cl, pc, flags, traces), [SIX, SIX16, SIX16, MSG], [blocks(6, BF16)] * 2,
        target=target,
    )
    from_prev1 = shift(msg_g1, 1)
    b1, d1, a1, b1h, b1l, d1h, d1l, a1h, a1l, traces1 = call(
        next_rest, 24, (from_prev, xb, xd, xa, pb, pd, pa, c1, flags, traces), [SIX] * 3 + [SIX16] * 6 + [TRACES],
        target=target,
    )

    traces1, (pa1, pb1, pd1, pc1) = total(
        traces1,
        [
            lambda r: call(product_a, 8, (a1h, a1l, c1h, c1l, d1h, d1l, r), SIX, specs={6: ANY}),
            lambda r: call(product_b, 8, (b1h, b1l, d1h, d1l, r), SIX, specs={4: ANY}),
            lambda r: call(product_d, 8, (b1h, b1l, d1h, d1l, a1h, a1l, r), SIX, specs={6: ANY}),
            lambda r: call(product_c, 8, (a1h, a1l, c1h, c1l, r), SIX, specs={4: ANY}),
        ],
    )
    pc1 = call(
        across, 12, (next_block, next_e, msg_g, c1h, c1l, pc1, traces, traces1), SIX, [blocks(6, BF16)] * 2, {7: ANY},
        target=target,
    )
    out = jax.ShapeDtypeStruct(stored.shape, F32)
    most = call(
        finish_most, 16, (pa1, pc1, pd1, a1, c1, d1, flags, traces1), out, [blocks(18), DMA((18,))], None, HBM,
        target=target,
    )
    return call(
        finish_b, 8, (most, from_prev1, pb1, b1, flags, traces1), out, [blocks(6), DMA((6,))], {0: HBM}, HBM, {0: 0},
        target,
    )


def solution(mesh):
    in_specs = (P(AXES, None, None, None), P(AXES, None))
    out_specs = P(AXES, None, None, None)
    return jax.shard_map(local, mesh=mesh, in_specs=in_specs, out_specs=out_specs, check_vma=False)
```

```python
import functools

import jax
import jax.numpy as jnp
from jax import lax
from jax.experimental import pallas as pl
from jax.experimental.pallas import tpu as pltpu
from jax.sharding import PartitionSpec as P

BS = 256
HALF = 128
AXES = ("row", "col")
UPPER = ((0, 0), (0, 1), (0, 2), (1, 1), (1, 2), (2, 2))
LOWER = ((0, 0), (1, 0), (1, 1), (2, 0), (2, 1), (2, 2))
OFFDIAG = ((0, 1), (0, 2), (1, 2))
PACKED = 3 * 512 + 3 * 256 + 8
F32 = jnp.float32
BF16 = jnp.bfloat16


def at_b(r, c):
    return r, c - r


def at_a(r, c):
    return 3 + r, c - r


def at_d(r, c):
    return r, 3 + c - r


def at_c(r, c):
    return 3 + r, 3 + c - r


def weights(traces, target):
    def all_of(x):
        return jnp.sum(jnp.sum(x, axis=0, keepdims=True), axis=1, keepdims=True)

    one, two = all_of(traces[0:8, :]), all_of(traces[8:16, :])
    mixing = (target - two) / (2.0 * (one - two))
    return 1.0 - 2.0 * mixing, 2.0 * mixing


def flag(flags, place):
    return flags[place[0] : place[0] + 1, place[1] : place[1] + 1]


def split(x):
    hi = x.astype(BF16)
    return hi, (x - hi.astype(F32)).astype(BF16)


def grid2(n):
    return lax.broadcasted_iota(jnp.int32, (n, n), 0), lax.broadcasted_iota(jnp.int32, (n, n), 1)


def symmetric(x):
    return 0.5 * (x + x.T)


def present(pattern, rd):
    return pattern[rd[1], rd[0]].astype(F32)


def pack(msg, blocks, flags):
    for n, rc in enumerate(OFFDIAG):
        x = blocks(rc)
        msg[512 * n : 512 * n + 256, :] = x[:, :HALF]
        msg[512 * n + 256 : 512 * n + 512, :] = x[:, HALF:]
    rows, cols = grid2(HALF)
    tail = []
    for r in range(3):
        x = blocks((r, r))
        base = 1536 + 256 * r
        first, second = x[:HALF, :HALF], x[HALF:, HALF:]
        msg[base : base + HALF, :] = x[:HALF, HALF:]
        msg[base + HALF : base + 256, :] = jnp.where(rows <= cols, first, second)
        tail.append(jnp.sum(jnp.where(rows == cols, second, 0.0), axis=0, keepdims=True))
    for f in flags:
        tail.append(jnp.full((1, HALF), f, F32))
    tail.append(jnp.zeros((8 - len(tail), HALF), F32))
    msg[2304:2312, :] = jnp.concatenate(tail, axis=0)


def unpack_off(msg, n):
    return jnp.concatenate([msg[512 * n : 512 * n + 256, :], msg[512 * n + 256 : 512 * n + 512, :]], axis=1)


def unpack_diag(msg, r):
    rows, cols = grid2(HALF)
    base = 1536 + 256 * r
    corner = msg[base : base + HALF, :]
    both = msg[base + HALF : base + 256, :]
    flipped = both.T
    line = msg[2304 + r : 2305 + r, :]
    first = jnp.where(rows <= cols, both, flipped)
    second = jnp.where(rows > cols, both, flipped)
    second = jnp.where(rows == cols, line, second)
    return jnp.concatenate(
        [jnp.concatenate([first, corner], axis=1), jnp.concatenate([corner.T, second], axis=1)], axis=0
    )


def unpack(msg, rc):
    return unpack_diag(msg, rc[0]) if rc[0] == rc[1] else unpack_off(msg, OFFDIAG.index(rc))


def flag_of(msg, rc):
    n = OFFDIAG.index(rc)
    return msg[2307 + n : 2308 + n, 0:1]


def upper(hl, r, c):
    hi, lo = hl
    if r <= c:
        n = UPPER.index((r, c))
        return hi[n], lo[n], False
    n = UPPER.index((c, r))
    return hi[n], lo[n], True


def lower(hl, r, c):
    n = LOWER.index((r, c))
    return hl[0][n], hl[1][n], False


def flipped(x):
    return x[0], x[1], not x[2]


def multiply(x, y):
    dims = (((0 if x[2] else 1,), (1 if y[2] else 0,)), ((), ()))

    def dot(p, q):
        return lax.dot_general(p, q, dims, preferred_element_type=F32)

    return dot(x[0], y[0]) + (dot(x[0], y[1]) + dot(x[1], y[0]))


def add_up(pairs):
    total = None
    for x, y in pairs:
        product = multiply(x, y)
        total = product if total is None else total + product
    return total


def gram(c):
    return {
        (r, s): add_up((flipped(lower(c, k, r)), lower(c, k, s)) for k in range(s, 3)) for r, s in UPPER
    }


def fetch(stored, places, buffer, sems):
    copies = [
        pltpu.make_async_copy(stored.at[r, d], buffer.at[n], sems.at[n]) for n, (r, d) in enumerate(places)
    ]
    for copy in copies:
        copy.start()
    return copies


def squares(x):
    y = jnp.sum((x * x).reshape(32, 8, BS), axis=0)
    return y[:, :HALF] + y[:, HALF:]


def diagonals(x):
    rows, cols = grid2(BS)
    y = jnp.sum(jnp.where(rows == cols, x, 0.0).reshape(32, 8, BS), axis=0)
    return y[:, :HALF] + y[:, HALF:]


class Traces:
    def __init__(self):
        self.one = jnp.zeros((8, HALF), F32)
        self.two = jnp.zeros((8, HALF), F32)

    def add(self, x, place):
        if place[1] == 0:
            self.one = self.one + diagonals(x)
            self.two = self.two + squares(x)
        else:
            self.two = self.two + 2.0 * squares(x)

    def write(self, ref):
        ref[0:8, :] = self.one
        ref[8:16, :] = self.two


def pack_b(stored, whole_pattern, msg, token, buffer, pattern, sems, pattern_sem):
    copies = fetch(stored, [at_b(*rc) for rc in UPPER], buffer, sems)
    flags = pltpu.make_async_copy(whole_pattern, pattern, pattern_sem)
    flags.start()
    flags.wait()

    def block(rc):
        n = UPPER.index(rc)
        copies[n].wait()
        x = buffer[n]
        return symmetric(x) if rc[0] == rc[1] else x * present(pattern, at_b(*rc))

    pack(msg, block, [present(pattern, at_b(*rc)) for rc in OFFDIAG])
    token[...] = msg[2304:2312, :]


GROUPS = (("c", LOWER, at_c), ("a", UPPER, at_a), ("d", LOWER, at_d), ("b", UPPER, at_b))
PLACES = [at(*rc) for _, order, at in GROUPS for rc in order]


def prepare(
    stored, whole_pattern, dep, xc, xa, xd, xb, ch, cl, ah, al, dh, dl, bh, bl, msg, traces, flags, buffer, pattern,
    sems, pattern_sem,
):
    del dep
    copies = fetch(stored, PLACES, buffer, sems)
    copy = pltpu.make_async_copy(whole_pattern, pattern, pattern_sem)
    copy.start()
    copy.wait()
    rows, cols = (lax.broadcasted_iota(jnp.int32, (8, HALF), n) for n in (0, 1))
    table = jnp.zeros((8, HALF), F32)
    for place in PLACES:
        table = jnp.where((rows == place[0]) & (cols == place[1]), present(pattern, place), table)
    flags[...] = table
    t = Traces()
    for g, (x_ref, hi, lo) in enumerate(((xc, ch, cl), (xa, ah, al), (xd, dh, dl), (xb, bh, bl))):
        for n in range(6):
            k = 6 * g + n
            place = PLACES[k]
            copies[k].wait()
            x = buffer[k]
            x = symmetric(x) if place[1] == 0 else x * present(pattern, place)
            x_ref[n] = x
            hi[n], lo[n] = split(x)
            t.add(x, place)
        if g == 0:
            products = gram((ch, cl))
            pack(msg, lambda rc: products[rc], [])
    t.write(traces)


def product_c(ah, al, ch, cl, dep, pc):
    del dep
    a, c = (ah, al), (ch, cl)
    for n, (r, s) in enumerate(LOWER):
        pc[n] = add_up((upper(a, r, k), lower(c, k, s)) for k in range(s, 3))


def product_a(ah, al, ch, cl, dh, dl, dep, pa):
    del dep
    a, c, d = (ah, al), (ch, cl), (dh, dl)
    for n, (r, s) in enumerate(UPPER):
        pairs = [(flipped(lower(d, k, r)), lower(d, k, s)) for k in range(s, 3)]
        pairs += [(upper(a, r, k), upper(a, k, s)) for k in range(3)]
        pairs += [(lower(c, r, k), flipped(lower(c, s, k))) for k in range(r + 1)]
        pa[n] = add_up(pairs)


def own_b(b, d, r, s):
    pairs = [(upper(b, r, k), upper(b, k, s)) for k in range(3)]
    pairs += [(lower(d, r, k), flipped(lower(d, s, k))) for k in range(r + 1)]
    return add_up(pairs)


def product_b(bh, bl, dh, dl, dep, pb):
    del dep
    for n, (r, s) in enumerate(UPPER):
        pb[n] = own_b((bh, bl), (dh, dl), r, s)


def product_b_packed(bh, bl, dh, dl, dep, pb, msg):
    del dep
    for n, (r, s) in enumerate(UPPER):
        pb[n] = own_b((bh, bl), (dh, dl), r, s)
    pack(msg, lambda rc: pb[UPPER.index(rc)], [])


def product_d(bh, bl, dh, dl, ah, al, dep, pd):
    del dep
    a, b, d = (ah, al), (bh, bl), (dh, dl)
    for n, (r, s) in enumerate(LOWER):
        pairs = [(upper(b, r, k), lower(d, k, s)) for k in range(s, 3)]
        pairs += [(lower(d, r, k), upper(a, k, s)) for k in range(r + 1)]
        pd[n] = add_up(pairs)


def next_c(target, msg_b, xc, ch, cl, pc, flags, traces, c1, c1h, c1l, msg_g, bh, bl):
    for n, rc in enumerate(UPPER):
        bh[n], bl[n] = split(unpack(msg_b, rc))
    a, b = weights(traces, target)
    old, nb = (ch, cl), (bh, bl)
    for n, (r, s) in enumerate(LOWER):
        p = pc[n] + add_up((lower(old, r, k), upper(nb, k, s)) for k in range(r + 1))
        x = (a * flag(flags, at_c(r, s))) * p + b * xc[n]
        c1[n] = x
        c1h[n], c1l[n] = split(x)
    products = gram((c1h, c1l))
    pack(msg_g, lambda rc: products[rc], [])


def next_rest(
    target, msg_g, xb, xd, xa, pb, pd, pa, c1, flags, old_traces, b1, d1, a1, b1h, b1l, d1h, d1l, a1h, a1l, traces
):
    a, b = weights(old_traces, target)
    t = Traces()
    work = (
        (xa, pa, a1, a1h, a1l, UPPER, at_a),
        (xd, pd, d1, d1h, d1l, LOWER, at_d),
        (xb, pb, b1, b1h, b1l, UPPER, at_b),
    )
    for old, product, new, hi, lo, order, at in work:
        for n, rc in enumerate(order):
            place = at(*rc)
            p = product[n]
            if at is at_b:
                p = p + unpack(msg_g, rc)
            scale = a if place[1] == 0 else a * flag(flags, place)
            x = scale * p + b * old[n]
            new[n] = x
            hi[n], lo[n] = split(x)
            t.add(x, place)
    for n, rc in enumerate(LOWER):
        t.add(c1[n], at_c(*rc))
    t.write(traces)


def finish_c(target, base, msg_b, msg_e, msg_g, c1, c1h, c1l, pc1, flags, traces, traces1, out, nh, nl, buffer, sems):
    del base
    a, b = weights(traces, target)
    for n, rc in enumerate(UPPER):
        p = unpack(msg_e, rc) + unpack(msg_g, rc)
        if rc[0] != rc[1]:
            p = p * flag_of(msg_b, rc)
        nh[n], nl[n] = split(a * p + b * unpack(msg_b, rc))
    c, nb = (c1h, c1l), (nh, nl)
    a, b = weights(traces1, target)
    copies = []
    for n, (r, s) in enumerate(LOWER):
        place = at_c(r, s)
        p = pc1[n] + add_up((lower(c, r, k), upper(nb, k, s)) for k in range(r + 1))
        buffer[n] = (a * flag(flags, place)) * p + b * c1[n]
        copies.append(pltpu.make_async_copy(buffer.at[n], out.at[place[0], place[1]], sems.at[n]))
        copies[-1].start()
    for copy in copies:
        copy.wait()


def finish_ad(target, pa1, pd1, a1, d1, flags, traces, out, buffer, sems):
    a, b = weights(traces, target)
    copies = []
    groups = ((pd1, d1, LOWER, at_d), (pa1, a1, UPPER, at_a))
    for p, x, order, at in groups:
        for n, rc in enumerate(order):
            place = at(*rc)
            k = len(copies)
            scale = a if place[1] == 0 else a * flag(flags, place)
            buffer[k] = scale * p[n] + b * x[n]
            copies.append(pltpu.make_async_copy(buffer.at[k], out.at[place[0], place[1]], sems.at[k]))
            copies[-1].start()
    for copy in copies:
        copy.wait()


def finish_b(target, base, msg_g, pb1, b1, flags, traces, out, buffer, sems):
    del base
    a, b = weights(traces, target)
    copies = []
    for n, rc in enumerate(UPPER):
        place = at_b(*rc)
        scale = a if place[1] == 0 else a * flag(flags, place)
        buffer[n] = scale * (pb1[n] + unpack(msg_g, rc)) + b * b1[n]
        copies.append(pltpu.make_async_copy(buffer.at[n], out.at[place[0], place[1]], sems.at[n]))
        copies[-1].start()
    for copy in copies:
        copy.wait()


HBM = pl.BlockSpec(memory_space=pltpu.HBM)
ANY = pl.BlockSpec(memory_space=pl.ANY)
VMEM = pl.BlockSpec(memory_space=pltpu.VMEM)
MSG = jax.ShapeDtypeStruct((PACKED, HALF), F32)
SIX = jax.ShapeDtypeStruct((6, BS, BS), F32)
SIX16 = jax.ShapeDtypeStruct((6, BS, BS), BF16)
TRACES = jax.ShapeDtypeStruct((16, HALF), F32)
FLAGS = jax.ShapeDtypeStruct((8, HALF), F32)
PATTERN = [pltpu.SMEM((4, 6), jnp.int32)]
DMA = pltpu.SemaphoreType.DMA


def blocks(n, dtype=F32):
    return pltpu.VMEM((n, BS, BS), dtype)


def call(body, limit, ins, outs, scratch=(), specs=None, out_spec=VMEM, aliases=None, target=None):
    many = isinstance(outs, (list, tuple))
    in_specs = [(specs or {}).get(n, VMEM) for n in range(len(ins))]
    return pl.pallas_call(
        body if target is None else functools.partial(body, target),
        out_shape=outs,
        in_specs=in_specs,
        out_specs=[out_spec] * len(outs) if many else out_spec,
        scratch_shapes=list(scratch),
        input_output_aliases=aliases or {},
        cost_estimate=pl.CostEstimate(flops=1024, bytes_accessed=1024, transcendentals=0),
        compiler_params=pltpu.CompilerParams(vmem_limit_bytes=limit * 2**20),
        name=getattr(body, "__name__", "add_arrays"),
    )(*ins)


def shift(x, step):
    count = lax.axis_size(AXES)
    pairs = [(i, i + step) for i in range(count) if 0 <= i + step < count]
    return lax.ppermute(x, AXES, pairs)


def place_of(i):
    return i // 2 % 4, i // 32, i // 16 % 2 * 2 + i % 2, i // 8 % 2


def index_of(x, y, z, core):
    return ((y % 4 * 2 + z % 4 // 2) * 2 + core % 2) * 8 + x % 4 * 2 + z % 2


def add_arrays(count, *refs):
    total = refs[0][...]
    for ref in refs[1:count]:
        total = total + ref[...]
    refs[-1][...] = total


def total(x, kernels):
    kernels = list(kernels)
    results = []
    count = lax.axis_size(AXES)

    def moved(v, f):
        return lax.ppermute(v, AXES, [(i, f(i)) for i in range(count)])

    def by(f):
        return lambda i: index_of(*f(*place_of(i)))

    def finished(x, arrived):
        ins = [x, *arrived]
        specs = {}
        if kernels:
            results.append(kernels.pop(0)(x))
            last = results[-1]
            specs[len(ins)] = ANY
            ins.append(last[0] if isinstance(last, (list, tuple)) else last)
        return call(functools.partial(add_arrays, 1 + len(arrived)), 1, ins, TRACES, specs=specs)

    if (lax.axis_size("row"), lax.axis_size("col")) != (16, 8):
        for k in range(count.bit_length() - 1):
            x = finished(x, [moved(x, lambda i: i ^ (1 << k))])
    else:
        x = finished(x, [moved(x, by(lambda x, y, z, c: (x, y + k, z + k, c))) for k in (1, 2, 3)])
        x = finished(x, [moved(x, by(lambda x, y, z, c: (x, y + k, z, c))) for k in (1, 2, 3)])
        x = finished(x, [moved(x, by(lambda x, y, z, c: (x, y, z, c + 1)))])

        def ahead(x, z):
            return x + (1 if z % 2 == 0 else -1)

        near = moved(x, by(lambda x, y, z, c: (ahead(x, z), y, z, c)))
        other = moved(x, by(lambda x, y, z, c: (ahead(x, z), y, z // 2 * 2 + 1 - z % 2, c)))
        x = finished(x, [near, other])
        x = finished(x, [moved(near, by(lambda x, y, z, c: (ahead(x, z), y, z, c)))])
    while kernels:
        results.append(kernels.pop(0)(x))
    return x, results


def local(stored, pattern):
    target = float(stored.shape[0] * lax.axis_size(AXES) * stored.shape[2] * 2 // 5)

    pattern = pattern.T
    msg_b, token = call(
        pack_b, 55, (stored, pattern), [MSG, FLAGS], [blocks(6), *PATTERN, DMA((6,)), DMA(())], {0: HBM, 1: HBM}
    )
    next_block = shift(msg_b, -1)
    xc, xa, xd, xb, ch, cl, ah, al, dh, dl, bh, bl, msg_g, traces, flags = call(
        prepare, 40, (stored, pattern, token), [SIX] * 4 + [SIX16] * 8 + [MSG, TRACES, FLAGS],
        [blocks(24), *PATTERN, DMA((24,)), DMA(())], {0: HBM, 1: HBM, 2: ANY},
    )
    from_prev = shift(msg_g, 1)

    traces, (pc, pa, (pb, msg_e), pd) = total(
        traces,
        [
            lambda r: call(product_c, 8, (ah, al, ch, cl, r), SIX, specs={4: ANY}),
            lambda r: call(product_a, 8, (ah, al, ch, cl, dh, dl, r), SIX, specs={6: ANY}),
            lambda r: call(product_b_packed, 8, (bh, bl, dh, dl, r), [SIX, MSG], specs={4: ANY}),
            lambda r: call(product_d, 8, (bh, bl, dh, dl, ah, al, r), SIX, specs={6: ANY}),
        ],
    )

    msg_e, _, _ = lax.optimization_barrier((msg_e, next_block, traces))
    next_e = shift(msg_e, -1)
    c1, c1h, c1l, msg_g1 = call(
        next_c, 14, (next_block, xc, ch, cl, pc, flags, traces), [SIX, SIX16, SIX16, MSG], [blocks(6, BF16)] * 2,
        target=target,
    )
    from_prev1 = shift(msg_g1, 1)
    b1, d1, a1, b1h, b1l, d1h, d1l, a1h, a1l, traces1 = call(
        next_rest, 24, (from_prev, xb, xd, xa, pb, pd, pa, c1, flags, traces), [SIX] * 3 + [SIX16] * 6 + [TRACES],
        target=target,
    )

    traces1, (pa1, pb1, pd1, pc1) = total(
        traces1,
        [
            lambda r: call(product_a, 8, (a1h, a1l, c1h, c1l, d1h, d1l, r), SIX, specs={6: ANY}),
            lambda r: call(product_b, 8, (b1h, b1l, d1h, d1l, r), SIX, specs={4: ANY}),
            lambda r: call(product_d, 8, (b1h, b1l, d1h, d1l, a1h, a1l, r), SIX, specs={6: ANY}),
            lambda r: call(product_c, 8, (a1h, a1l, c1h, c1l, r), SIX, specs={4: ANY}),
        ],
    )
    out = jax.ShapeDtypeStruct(stored.shape, F32)
    done = call(
        finish_ad, 12, (pa1, pd1, a1, d1, flags, traces1), out, [blocks(12), DMA((12,))], None, HBM, target=target
    )
    done = call(
        finish_c, 14, (done, next_block, next_e, msg_g, c1, c1h, c1l, pc1, flags, traces, traces1), out,
        [blocks(6, BF16)] * 2 + [blocks(6), DMA((6,))], {0: HBM}, HBM, {0: 0}, target,
    )
    return call(
        finish_b, 8, (done, from_prev1, pb1, b1, flags, traces1), out, [blocks(6), DMA((6,))], {0: HBM}, HBM, {0: 0},
        target,
    )


def solution(mesh):
    in_specs = (P(AXES, None, None, None), P(AXES, None))
    out_specs = P(AXES, None, None, None)
    return jax.shard_map(local, mesh=mesh, in_specs=in_specs, out_specs=out_specs, check_vma=False)
```

```python
import functools

import jax
import jax.numpy as jnp
from jax import lax
from jax.experimental import pallas as pl
from jax.experimental.pallas import tpu as pltpu
from jax.sharding import PartitionSpec as P

BS = 256
HALF = 128
AXES = ("row", "col")
UPPER = ((0, 0), (0, 1), (0, 2), (1, 1), (1, 2), (2, 2))
LOWER = ((0, 0), (1, 0), (1, 1), (2, 0), (2, 1), (2, 2))
OFFDIAG = ((0, 1), (0, 2), (1, 2))
PACKED = 3 * 512 + 3 * 256 + 8
F32 = jnp.float32
BF16 = jnp.bfloat16


def at_b(r, c):
    return r, c - r


def at_a(r, c):
    return 3 + r, c - r


def at_d(r, c):
    return r, 3 + c - r


def at_c(r, c):
    return 3 + r, 3 + c - r


def weights(traces, target):
    def all_of(x):
        return jnp.sum(jnp.sum(x, axis=0, keepdims=True), axis=1, keepdims=True)

    one, two = all_of(traces[0:8, :]), all_of(traces[8:16, :])
    mixing = (target - two) / (2.0 * (one - two))
    return 1.0 - 2.0 * mixing, 2.0 * mixing


def flag(flags, place):
    return flags[place[0] : place[0] + 1, place[1] : place[1] + 1]


def split(x):
    hi = x.astype(BF16)
    return hi, (x - hi.astype(F32)).astype(BF16)


def grid2(n):
    return lax.broadcasted_iota(jnp.int32, (n, n), 0), lax.broadcasted_iota(jnp.int32, (n, n), 1)


def symmetric(x):
    return 0.5 * (x + x.T)


def present(pattern, rd):
    return pattern[rd[1], rd[0]].astype(F32)


def pack(msg, blocks, flags):
    for n, rc in enumerate(OFFDIAG):
        x = blocks(rc)
        msg[512 * n : 512 * n + 256, :] = x[:, :HALF]
        msg[512 * n + 256 : 512 * n + 512, :] = x[:, HALF:]
    rows, cols = grid2(HALF)
    tail = []
    for r in range(3):
        x = blocks((r, r))
        base = 1536 + 256 * r
        first, second = x[:HALF, :HALF], x[HALF:, HALF:]
        msg[base : base + HALF, :] = x[:HALF, HALF:]
        msg[base + HALF : base + 256, :] = jnp.where(rows <= cols, first, second)
        tail.append(jnp.sum(jnp.where(rows == cols, second, 0.0), axis=0, keepdims=True))
    for f in flags:
        tail.append(jnp.full((1, HALF), f, F32))
    tail.append(jnp.zeros((8 - len(tail), HALF), F32))
    msg[2304:2312, :] = jnp.concatenate(tail, axis=0)


def unpack_off(msg, n):
    return jnp.concatenate([msg[512 * n : 512 * n + 256, :], msg[512 * n + 256 : 512 * n + 512, :]], axis=1)


def unpack_diag(msg, r):
    rows, cols = grid2(HALF)
    base = 1536 + 256 * r
    corner = msg[base : base + HALF, :]
    both = msg[base + HALF : base + 256, :]
    flipped = both.T
    line = msg[2304 + r : 2305 + r, :]
    first = jnp.where(rows <= cols, both, flipped)
    second = jnp.where(rows > cols, both, flipped)
    second = jnp.where(rows == cols, line, second)
    return jnp.concatenate(
        [jnp.concatenate([first, corner], axis=1), jnp.concatenate([corner.T, second], axis=1)], axis=0
    )


class Either:
    def __init__(self, one, other):
        self.one, self.other = one, other

    def __getitem__(self, where):
        return self.one[where] + self.other[where]


def unpack(msg, rc):
    return unpack_diag(msg, rc[0]) if rc[0] == rc[1] else unpack_off(msg, OFFDIAG.index(rc))


def flag_of(msg, rc):
    n = OFFDIAG.index(rc)
    return msg[2307 + n : 2308 + n, 0:1]


def upper(hl, r, c):
    hi, lo = hl
    if r <= c:
        n = UPPER.index((r, c))
        return hi[n], lo[n], False
    n = UPPER.index((c, r))
    return hi[n], lo[n], True


def lower(hl, r, c):
    n = LOWER.index((r, c))
    return hl[0][n], hl[1][n], False


def flipped(x):
    return x[0], x[1], not x[2]


def multiply(x, y):
    dims = (((0 if x[2] else 1,), (1 if y[2] else 0,)), ((), ()))

    def dot(p, q):
        return lax.dot_general(p, q, dims, preferred_element_type=F32)

    return dot(x[0], y[0]) + (dot(x[0], y[1]) + dot(x[1], y[0]))


def add_up(pairs):
    total = None
    for x, y in pairs:
        product = multiply(x, y)
        total = product if total is None else total + product
    return total


def gram(c):
    return {
        (r, s): add_up((flipped(lower(c, k, r)), lower(c, k, s)) for k in range(s, 3)) for r, s in UPPER
    }


def fetch(stored, places, buffer, sems):
    copies = [
        pltpu.make_async_copy(stored.at[r, d], buffer.at[n], sems.at[n]) for n, (r, d) in enumerate(places)
    ]
    for copy in copies:
        copy.start()
    return copies


def squares(x):
    y = jnp.sum((x * x).reshape(32, 8, BS), axis=0)
    return y[:, :HALF] + y[:, HALF:]


def diagonals(x):
    rows, cols = grid2(BS)
    y = jnp.sum(jnp.where(rows == cols, x, 0.0).reshape(32, 8, BS), axis=0)
    return y[:, :HALF] + y[:, HALF:]


class Traces:
    def __init__(self):
        self.one = jnp.zeros((8, HALF), F32)
        self.two = jnp.zeros((8, HALF), F32)

    def add(self, x, place):
        if place[1] == 0:
            self.one = self.one + diagonals(x)
            self.two = self.two + squares(x)
        else:
            self.two = self.two + 2.0 * squares(x)

    def write(self, ref):
        ref[0:8, :] = self.one
        ref[8:16, :] = self.two


def pack_b(stored, whole_pattern, msg, token, buffer, pattern, sems, pattern_sem):
    copies = fetch(stored, [at_b(*rc) for rc in UPPER], buffer, sems)
    flags = pltpu.make_async_copy(whole_pattern, pattern, pattern_sem)
    flags.start()
    flags.wait()

    def block(rc):
        n = UPPER.index(rc)
        copies[n].wait()
        x = buffer[n]
        return symmetric(x) if rc[0] == rc[1] else x * present(pattern, at_b(*rc))

    pack(msg, block, [present(pattern, at_b(*rc)) for rc in OFFDIAG])
    token[...] = msg[2304:2312, :]


GROUPS = (("c", LOWER, at_c), ("a", UPPER, at_a), ("d", LOWER, at_d), ("b", UPPER, at_b))
PLACES = [at(*rc) for _, order, at in GROUPS for rc in order]


def prepare(
    stored, whole_pattern, dep, xc, xa, xd, xb, ch, cl, ah, al, dh, dl, bh, bl, msg, traces, flags, buffer, pattern,
    sems, pattern_sem,
):
    del dep
    copies = fetch(stored, PLACES, buffer, sems)
    copy = pltpu.make_async_copy(whole_pattern, pattern, pattern_sem)
    copy.start()
    copy.wait()
    rows, cols = (lax.broadcasted_iota(jnp.int32, (8, HALF), n) for n in (0, 1))
    table = jnp.zeros((8, HALF), F32)
    for place in PLACES:
        table = jnp.where((rows == place[0]) & (cols == place[1]), present(pattern, place), table)
    flags[...] = table
    t = Traces()
    for g, (x_ref, hi, lo) in enumerate(((xc, ch, cl), (xa, ah, al), (xd, dh, dl), (xb, bh, bl))):
        for n in range(6):
            k = 6 * g + n
            place = PLACES[k]
            copies[k].wait()
            x = buffer[k]
            x = symmetric(x) if place[1] == 0 else x * present(pattern, place)
            x_ref[n] = x
            hi[n], lo[n] = split(x)
            t.add(x, place)
        if g == 0:
            products = gram((ch, cl))
            pack(msg, lambda rc: products[rc], [])
    t.write(traces)


def product_c(ah, al, ch, cl, dep, pc):
    del dep
    a, c = (ah, al), (ch, cl)
    for n, (r, s) in enumerate(LOWER):
        pc[n] = add_up((upper(a, r, k), lower(c, k, s)) for k in range(s, 3))


def product_a(ah, al, ch, cl, dh, dl, dep, pa):
    del dep
    a, c, d = (ah, al), (ch, cl), (dh, dl)
    for n, (r, s) in enumerate(UPPER):
        pairs = [(flipped(lower(d, k, r)), lower(d, k, s)) for k in range(s, 3)]
        pairs += [(upper(a, r, k), upper(a, k, s)) for k in range(3)]
        pairs += [(lower(c, r, k), flipped(lower(c, s, k))) for k in range(r + 1)]
        pa[n] = add_up(pairs)


def own_b(b, d, r, s):
    pairs = [(upper(b, r, k), upper(b, k, s)) for k in range(3)]
    pairs += [(lower(d, r, k), flipped(lower(d, s, k))) for k in range(r + 1)]
    return add_up(pairs)


def product_b(bh, bl, dh, dl, dep, pb):
    del dep
    for n, (r, s) in enumerate(UPPER):
        pb[n] = own_b((bh, bl), (dh, dl), r, s)


def product_b_packed(bh, bl, dh, dl, dep, pb, msg):
    del dep
    for n, (r, s) in enumerate(UPPER):
        pb[n] = own_b((bh, bl), (dh, dl), r, s)
    pack(msg, lambda rc: pb[UPPER.index(rc)], [])


def product_d(bh, bl, dh, dl, ah, al, dep, pd):
    del dep
    a, b, d = (ah, al), (bh, bl), (dh, dl)
    for n, (r, s) in enumerate(LOWER):
        pairs = [(upper(b, r, k), lower(d, k, s)) for k in range(s, 3)]
        pairs += [(lower(d, r, k), upper(a, k, s)) for k in range(r + 1)]
        pd[n] = add_up(pairs)


def next_c(target, msg_b, xc, ch, cl, pc, flags, traces, c1, c1h, c1l, msg_g, bh, bl):
    for n, rc in enumerate(UPPER):
        bh[n], bl[n] = split(unpack(msg_b, rc))
    a, b = weights(traces, target)
    old, nb = (ch, cl), (bh, bl)
    for n, (r, s) in enumerate(LOWER):
        p = pc[n] + add_up((lower(old, r, k), upper(nb, k, s)) for k in range(r + 1))
        x = (a * flag(flags, at_c(r, s))) * p + b * xc[n]
        c1[n] = x
        c1h[n], c1l[n] = split(x)
    products = gram((c1h, c1l))
    pack(msg_g, lambda rc: products[rc], [])


def next_rest(
    target, msg_g_even, msg_g_odd, xb, xd, xa, pb, pd, pa, c1, flags, old_traces, b1, d1, a1, b1h, b1l, d1h, d1l, a1h, a1l, traces
):
    msg_g = Either(msg_g_even, msg_g_odd)
    a, b = weights(old_traces, target)
    t = Traces()
    work = (
        (xa, pa, a1, a1h, a1l, UPPER, at_a),
        (xd, pd, d1, d1h, d1l, LOWER, at_d),
        (xb, pb, b1, b1h, b1l, UPPER, at_b),
    )
    for old, product, new, hi, lo, order, at in work:
        for n, rc in enumerate(order):
            place = at(*rc)
            p = product[n]
            if at is at_b:
                p = p + unpack(msg_g, rc)
            scale = a if place[1] == 0 else a * flag(flags, place)
            x = scale * p + b * old[n]
            new[n] = x
            hi[n], lo[n] = split(x)
            t.add(x, place)
    for n, rc in enumerate(LOWER):
        t.add(c1[n], at_c(*rc))
    t.write(traces)


def finish_ad(target, pa1, pd1, a1, d1, flags, traces, out, buffer, sems):
    a, b = weights(traces, target)
    copies = []
    groups = ((pd1, d1, LOWER, at_d), (pa1, a1, UPPER, at_a))
    for p, x, order, at in groups:
        for n, rc in enumerate(order):
            place = at(*rc)
            k = len(copies)
            scale = a if place[1] == 0 else a * flag(flags, place)
            buffer[k] = scale * p[n] + b * x[n]
            copies.append(pltpu.make_async_copy(buffer.at[k], out.at[place[0], place[1]], sems.at[k]))
            copies[-1].start()
    for copy in copies:
        copy.wait()


def write_blocks(out, buffer, sems, items):
    copies = []
    for place, x in items:
        k = len(copies)
        buffer[k] = x
        copies.append(pltpu.make_async_copy(buffer.at[k], out.at[place[0], place[1]], sems.at[k]))
        copies[-1].start()
    for copy in copies:
        copy.wait()


def finish_b(target, base, msg_g, pb1, b1, flags, traces, out, buffer, sems):
    del base
    a, b = weights(traces, target)

    def block(n, rc):
        place = at_b(*rc)
        scale = a if place[1] == 0 else a * flag(flags, place)
        return place, scale * (pb1[n] + unpack(msg_g, rc)) + b * b1[n]

    write_blocks(out, buffer, sems, (block(n, rc) for n, rc in enumerate(UPPER)))


def across(target, msg_b, msg_g, traces, dep, part, scales):
    del dep
    a, b = weights(traces, target)
    rows = []
    for n, rc in enumerate(UPPER):
        scale = a if rc[0] == rc[1] else a * flag_of(msg_b, rc)
        part[n] = scale * unpack(msg_g, rc) + b * unpack(msg_b, rc)
        rows.append(jnp.broadcast_to(scale, (1, HALF)))
    scales[...] = jnp.concatenate(rows + [jnp.zeros((2, HALF), F32)], axis=0)


def finish_c(
    target, base, msg_e_even, msg_e_odd, part, scales, c1, c1h, c1l, pc1, flags, traces, out, nh, nl, buffer, sems
):
    del base
    msg_e = Either(msg_e_even, msg_e_odd)
    for n, rc in enumerate(UPPER):
        nh[n], nl[n] = split(part[n] + scales[n : n + 1, 0:1] * unpack(msg_e, rc))
    c, nb = (c1h, c1l), (nh, nl)
    a, b = weights(traces, target)

    def block(n, r, s):
        p = pc1[n] + add_up((lower(c, r, k), upper(nb, k, s)) for k in range(r + 1))
        return at_c(r, s), (a * flag(flags, at_c(r, s))) * p + b * c1[n]

    write_blocks(out, buffer, sems, (block(n, r, s) for n, (r, s) in enumerate(LOWER)))


HBM = pl.BlockSpec(memory_space=pltpu.HBM)
ANY = pl.BlockSpec(memory_space=pl.ANY)
VMEM = pl.BlockSpec(memory_space=pltpu.VMEM)
MSG = jax.ShapeDtypeStruct((PACKED, HALF), F32)
SIX = jax.ShapeDtypeStruct((6, BS, BS), F32)
SIX16 = jax.ShapeDtypeStruct((6, BS, BS), BF16)
TRACES = jax.ShapeDtypeStruct((16, HALF), F32)
FLAGS = jax.ShapeDtypeStruct((8, HALF), F32)
PATTERN = [pltpu.SMEM((4, 6), jnp.int32)]
DMA = pltpu.SemaphoreType.DMA


def blocks(n, dtype=F32):
    return pltpu.VMEM((n, BS, BS), dtype)


def call(body, limit, ins, outs, scratch=(), specs=None, out_spec=VMEM, aliases=None, target=None):
    many = isinstance(outs, (list, tuple))
    in_specs = [(specs or {}).get(n, VMEM) for n in range(len(ins))]
    return pl.pallas_call(
        body if target is None else functools.partial(body, target),
        out_shape=outs,
        in_specs=in_specs,
        out_specs=[out_spec] * len(outs) if many else out_spec,
        scratch_shapes=list(scratch),
        input_output_aliases=aliases or {},
        cost_estimate=pl.CostEstimate(flops=1024, bytes_accessed=1024, transcendentals=0),
        compiler_params=pltpu.CompilerParams(vmem_limit_bytes=limit * 2**20),
        name=getattr(body, "__name__", "add_arrays"),
    )(*ins)


def shift(x, step, senders=(0, 1)):
    count = lax.axis_size(AXES)
    pairs = [(i, i + step) for i in range(count) if 0 <= i + step < count and i % 2 in senders]
    return lax.ppermute(x, AXES, pairs)


def place_of(i):
    return i // 2 % 4, i // 32, i // 16 % 2 * 2 + i % 2, i // 8 % 2


def index_of(x, y, z, core):
    return ((y % 4 * 2 + z % 4 // 2) * 2 + core % 2) * 8 + x % 4 * 2 + z % 2


def add_arrays(count, *refs):
    total = refs[0][...]
    for ref in refs[1:count]:
        total = total + ref[...]
    refs[-1][...] = total


def wait_for(x, arrived, same):
    del arrived
    same[...] = x[...]


def total(x, groups):
    groups = list(groups)
    results = []
    count = lax.axis_size(AXES)

    def moved(v, f):
        return lax.ppermute(v, AXES, [(i, f(i)) for i in range(count)])

    def by(f):
        return lambda i: index_of(*f(*place_of(i)))

    def finished(x, arrived):
        ins = [x, *arrived]
        specs = {}
        for kernel in groups.pop(0) if groups else ():
            results.append(kernel(x))
            last = results[-1]
            specs[len(ins)] = ANY
            ins.append(last[0] if isinstance(last, (list, tuple)) else last)
        return call(functools.partial(add_arrays, 1 + len(arrived)), 1, ins, TRACES, specs=specs)

    if (lax.axis_size("row"), lax.axis_size("col")) != (16, 8):
        for k in range(count.bit_length() - 1):
            x = finished(x, [moved(x, lambda i: i ^ (1 << k))])
    else:
        x = finished(x, [moved(x, by(lambda x, y, z, c: (x, y + k, z + k, c))) for k in (1, 2, 3)])
        x = finished(x, [moved(x, by(lambda x, y, z, c: (x, y + k, z, c))) for k in (1, 2, 3)])
        x = finished(x, [moved(x, by(lambda x, y, z, c: (x, y, z, c + 1)))])

        def ahead(x, z):
            return x + (1 if z % 2 == 0 else -1)

        near = moved(x, by(lambda x, y, z, c: (ahead(x, z), y, z, c)))
        other = moved(x, by(lambda x, y, z, c: (ahead(x, z), y, z // 2 * 2 + 1 - z % 2, c)))
        x = finished(x, [near, other])
        x = finished(x, [moved(near, by(lambda x, y, z, c: (ahead(x, z), y, z, c)))])
    for kernel in (kernel for group in groups for kernel in group):
        results.append(kernel(x))
    return x, results


def local(stored, pattern):
    target = float(stored.shape[0] * lax.axis_size(AXES) * stored.shape[2] * 2 // 5)

    pattern = pattern.T
    msg_b, token = call(
        pack_b, 55, (stored, pattern), [MSG, FLAGS], [blocks(6), *PATTERN, DMA((6,)), DMA(())], {0: HBM, 1: HBM}
    )
    next_block = shift(msg_b, -1)
    xc, xa, xd, xb, ch, cl, ah, al, dh, dl, bh, bl, msg_g, traces, flags = call(
        prepare, 40, (stored, pattern, token), [SIX] * 4 + [SIX16] * 8 + [MSG, TRACES, FLAGS],
        [blocks(24), *PATTERN, DMA((24,)), DMA(())], {0: HBM, 1: HBM, 2: ANY},
    )
    g_even = shift(msg_g, 1, (0,))
    traces, (pc, (pb, msg_e), pa, _) = total(
        traces,
        [
            [
                lambda r: call(product_c, 8, (ah, al, ch, cl, r), SIX, specs={4: ANY}),
                lambda r: call(product_b_packed, 8, (bh, bl, dh, dl, r), [SIX, MSG], specs={4: ANY}),
            ],
            [
                lambda r: call(product_a, 8, (ah, al, ch, cl, dh, dl, r), SIX, specs={6: ANY}),
            ],
            [lambda r: call(wait_for, 1, (r, next_block), TRACES, specs={1: ANY})],
        ],
    )
    e_odd = shift(msg_e, -1, (1,))
    late_g, _, _ = lax.optimization_barrier((msg_g, next_block, pa))
    g_odd = shift(late_g, 1, (1,))

    c1, c1h, c1l, msg_g1 = call(
        next_c, 14, (next_block, xc, ch, cl, pc, flags, traces), [SIX, SIX16, SIX16, MSG], [blocks(6, BF16)] * 2,
        target=target,
    )
    from_prev1 = shift(msg_g1, 1)
    pd = call(product_d, 8, (bh, bl, dh, dl, ah, al, c1), SIX, specs={6: ANY})
    late_e, _, _ = lax.optimization_barrier((msg_e, g_even, c1))
    e_even = shift(late_e, -1, (0,))
    b1, d1, a1, b1h, b1l, d1h, d1l, a1h, a1l, traces1 = call(
        next_rest, 24, (g_even, g_odd, xb, xd, xa, pb, pd, pa, c1, flags, traces), [SIX] * 3 + [SIX16] * 6 + [TRACES],
        target=target,
    )

    traces1, (pa1, pb1, pd1, pc1) = total(
        traces1,
        [
            [lambda r: call(product_a, 8, (a1h, a1l, c1h, c1l, d1h, d1l, r), SIX, specs={6: ANY})],
            [lambda r: call(product_b, 8, (b1h, b1l, d1h, d1l, r), SIX, specs={4: ANY})],
            [lambda r: call(product_d, 8, (b1h, b1l, d1h, d1l, a1h, a1l, r), SIX, specs={6: ANY})],
            [lambda r: call(product_c, 8, (a1h, a1l, c1h, c1l, r), SIX, specs={4: ANY})],
        ],
    )
    part, scales = call(
        across, 8, (next_block, msg_g, traces, traces1), [SIX, FLAGS], specs={3: ANY}, target=target
    )
    out = jax.ShapeDtypeStruct(stored.shape, F32)
    done = call(
        finish_ad, 12, (pa1, pd1, a1, d1, flags, traces1), out, [blocks(12), DMA((12,))], None, HBM, target=target
    )
    done = call(
        finish_b, 8, (done, from_prev1, pb1, b1, flags, traces1), out, [blocks(6), DMA((6,))], {0: HBM}, HBM, {0: 0},
        target,
    )
    return call(
        finish_c, 18, (done, e_even, e_odd, part, scales, c1, c1h, c1l, pc1, flags, traces1), out,
        [blocks(6, BF16)] * 2 + [blocks(6), DMA((6,))], {0: HBM}, HBM, {0: 0}, target,
    )


def solution(mesh):
    in_specs = (P(AXES, None, None, None), P(AXES, None))
    out_specs = P(AXES, None, None, None)
    return jax.shard_map(local, mesh=mesh, in_specs=in_specs, out_specs=out_specs, check_vma=False)
```

```python
import functools

import jax
import jax.numpy as jnp
from jax import lax
from jax.experimental import pallas as pl
from jax.experimental.pallas import tpu as pltpu
from jax.sharding import PartitionSpec as P

BS = 256
HALF = 128
AXES = ("row", "col")
UPPER = ((0, 0), (0, 1), (0, 2), (1, 1), (1, 2), (2, 2))
LOWER = ((0, 0), (1, 0), (1, 1), (2, 0), (2, 1), (2, 2))
OFFDIAG = ((0, 1), (0, 2), (1, 2))
PACKED = 3 * 512 + 3 * 256 + 8
F32 = jnp.float32
BF16 = jnp.bfloat16


def at_b(r, c):
    return r, c - r


def at_a(r, c):
    return 3 + r, c - r


def at_d(r, c):
    return r, 3 + c - r


def at_c(r, c):
    return 3 + r, 3 + c - r


def weights(traces, target):
    def all_of(x):
        return jnp.sum(jnp.sum(x, axis=0, keepdims=True), axis=1, keepdims=True)

    one, two = all_of(traces[0:8, :]), all_of(traces[8:16, :])
    mixing = (target - two) / (2.0 * (one - two))
    return 1.0 - 2.0 * mixing, 2.0 * mixing


def flag(flags, place):
    return flags[place[0] : place[0] + 1, place[1] : place[1] + 1]


def split(x):
    hi = x.astype(BF16)
    return hi, (x - hi.astype(F32)).astype(BF16)


def grid2(n):
    return lax.broadcasted_iota(jnp.int32, (n, n), 0), lax.broadcasted_iota(jnp.int32, (n, n), 1)


def symmetric(x):
    return 0.5 * (x + x.T)


def present(pattern, rd):
    return pattern[rd[1], rd[0]].astype(F32)


def pack(msg, blocks, flags):
    for n, rc in enumerate(OFFDIAG):
        x = blocks(rc)
        msg[512 * n : 512 * n + 256, :] = x[:, :HALF]
        msg[512 * n + 256 : 512 * n + 512, :] = x[:, HALF:]
    rows, cols = grid2(HALF)
    tail = []
    for r in range(3):
        x = blocks((r, r))
        base = 1536 + 256 * r
        first, second = x[:HALF, :HALF], x[HALF:, HALF:]
        msg[base : base + HALF, :] = x[:HALF, HALF:]
        msg[base + HALF : base + 256, :] = jnp.where(rows <= cols, first, second)
        tail.append(jnp.sum(jnp.where(rows == cols, second, 0.0), axis=0, keepdims=True))
    for f in flags:
        tail.append(jnp.full((1, HALF), f, F32))
    tail.append(jnp.zeros((8 - len(tail), HALF), F32))
    msg[2304:2312, :] = jnp.concatenate(tail, axis=0)


def unpack_off(msg, n):
    return jnp.concatenate([msg[512 * n : 512 * n + 256, :], msg[512 * n + 256 : 512 * n + 512, :]], axis=1)


def unpack_diag(msg, r):
    rows, cols = grid2(HALF)
    base = 1536 + 256 * r
    corner = msg[base : base + HALF, :]
    both = msg[base + HALF : base + 256, :]
    flipped = both.T
    line = msg[2304 + r : 2305 + r, :]
    first = jnp.where(rows <= cols, both, flipped)
    second = jnp.where(rows > cols, both, flipped)
    second = jnp.where(rows == cols, line, second)
    return jnp.concatenate(
        [jnp.concatenate([first, corner], axis=1), jnp.concatenate([corner.T, second], axis=1)], axis=0
    )


def unpack(msg, rc):
    return unpack_diag(msg, rc[0]) if rc[0] == rc[1] else unpack_off(msg, OFFDIAG.index(rc))


def flag_of(msg, rc):
    n = OFFDIAG.index(rc)
    return msg[2307 + n : 2308 + n, 0:1]


def upper(hl, r, c):
    hi, lo = hl
    if r <= c:
        n = UPPER.index((r, c))
        return hi[n], lo[n], False
    n = UPPER.index((c, r))
    return hi[n], lo[n], True


def lower(hl, r, c):
    n = LOWER.index((r, c))
    return hl[0][n], hl[1][n], False


def flipped(x):
    return x[0], x[1], not x[2]


def multiply(x, y):
    dims = (((0 if x[2] else 1,), (1 if y[2] else 0,)), ((), ()))

    def dot(p, q):
        return lax.dot_general(p, q, dims, preferred_element_type=F32)

    return dot(x[0], y[0]) + (dot(x[0], y[1]) + dot(x[1], y[0]))


def add_up(pairs):
    total = None
    for x, y in pairs:
        product = multiply(x, y)
        total = product if total is None else total + product
    return total


def gram(c):
    return {
        (r, s): add_up((flipped(lower(c, k, r)), lower(c, k, s)) for k in range(s, 3)) for r, s in UPPER
    }


def fetch(stored, places, buffer, sems):
    copies = [
        pltpu.make_async_copy(stored.at[r, d], buffer.at[n], sems.at[n]) for n, (r, d) in enumerate(places)
    ]
    for copy in copies:
        copy.start()
    return copies


def squares(x):
    y = jnp.sum((x * x).reshape(32, 8, BS), axis=0)
    return y[:, :HALF] + y[:, HALF:]


def diagonals(x):
    rows, cols = grid2(BS)
    y = jnp.sum(jnp.where(rows == cols, x, 0.0).reshape(32, 8, BS), axis=0)
    return y[:, :HALF] + y[:, HALF:]


class Traces:
    def __init__(self):
        self.one = jnp.zeros((8, HALF), F32)
        self.two = jnp.zeros((8, HALF), F32)

    def add(self, x, place):
        if place[1] == 0:
            self.one = self.one + diagonals(x)
            self.two = self.two + squares(x)
        else:
            self.two = self.two + 2.0 * squares(x)

    def write(self, ref):
        ref[0:8, :] = self.one
        ref[8:16, :] = self.two


def pack_b(stored, whole_pattern, msg, token, buffer, pattern, sems, pattern_sem):
    copies = fetch(stored, [at_b(*rc) for rc in UPPER], buffer, sems)
    flags = pltpu.make_async_copy(whole_pattern, pattern, pattern_sem)
    flags.start()
    flags.wait()

    def block(rc):
        n = UPPER.index(rc)
        copies[n].wait()
        x = buffer[n]
        return symmetric(x) if rc[0] == rc[1] else x * present(pattern, at_b(*rc))

    pack(msg, block, [present(pattern, at_b(*rc)) for rc in OFFDIAG])
    token[...] = msg[2304:2312, :]


GROUPS = (("c", LOWER, at_c), ("a", UPPER, at_a), ("d", LOWER, at_d), ("b", UPPER, at_b))
PLACES = [at(*rc) for _, order, at in GROUPS for rc in order]


def prepare(
    stored, whole_pattern, dep, xc, xa, xd, xb, ch, cl, ah, al, dh, dl, bh, bl, msg, traces, flags, buffer, pattern,
    sems, pattern_sem,
):
    del dep
    copies = fetch(stored, PLACES, buffer, sems)
    copy = pltpu.make_async_copy(whole_pattern, pattern, pattern_sem)
    copy.start()
    copy.wait()
    rows, cols = (lax.broadcasted_iota(jnp.int32, (8, HALF), n) for n in (0, 1))
    table = jnp.zeros((8, HALF), F32)
    for place in PLACES:
        table = jnp.where((rows == place[0]) & (cols == place[1]), present(pattern, place), table)
    flags[...] = table
    t = Traces()
    for g, (x_ref, hi, lo) in enumerate(((xc, ch, cl), (xa, ah, al), (xd, dh, dl), (xb, bh, bl))):
        for n in range(6):
            k = 6 * g + n
            place = PLACES[k]
            copies[k].wait()
            x = buffer[k]
            x = symmetric(x) if place[1] == 0 else x * present(pattern, place)
            x_ref[n] = x
            hi[n], lo[n] = split(x)
            t.add(x, place)
        if g == 0:
            products = gram((ch, cl))
            pack(msg, lambda rc: products[rc], [])
    t.write(traces)


def product_c(ah, al, ch, cl, dep, pc):
    del dep
    a, c = (ah, al), (ch, cl)
    for n, (r, s) in enumerate(LOWER):
        pc[n] = add_up((upper(a, r, k), lower(c, k, s)) for k in range(s, 3))


def product_a(ah, al, ch, cl, dh, dl, dep, pa):
    del dep
    a, c, d = (ah, al), (ch, cl), (dh, dl)
    for n, (r, s) in enumerate(UPPER):
        pairs = [(flipped(lower(d, k, r)), lower(d, k, s)) for k in range(s, 3)]
        pairs += [(upper(a, r, k), upper(a, k, s)) for k in range(3)]
        pairs += [(lower(c, r, k), flipped(lower(c, s, k))) for k in range(r + 1)]
        pa[n] = add_up(pairs)


def own_b(b, d, r, s):
    pairs = [(upper(b, r, k), upper(b, k, s)) for k in range(3)]
    pairs += [(lower(d, r, k), flipped(lower(d, s, k))) for k in range(r + 1)]
    return add_up(pairs)


def product_b(bh, bl, dh, dl, dep, pb):
    del dep
    for n, (r, s) in enumerate(UPPER):
        pb[n] = own_b((bh, bl), (dh, dl), r, s)


def product_b_packed(bh, bl, dh, dl, dep, pb, msg):
    del dep
    for n, (r, s) in enumerate(UPPER):
        pb[n] = own_b((bh, bl), (dh, dl), r, s)
    pack(msg, lambda rc: pb[UPPER.index(rc)], [])


def product_d(bh, bl, dh, dl, ah, al, dep, pd):
    del dep
    a, b, d = (ah, al), (bh, bl), (dh, dl)
    for n, (r, s) in enumerate(LOWER):
        pairs = [(upper(b, r, k), lower(d, k, s)) for k in range(s, 3)]
        pairs += [(lower(d, r, k), upper(a, k, s)) for k in range(r + 1)]
        pd[n] = add_up(pairs)


def next_c(target, msg_b, xc, ch, cl, pc, flags, traces, c1, c1h, c1l, msg_g, bh, bl):
    for n, rc in enumerate(UPPER):
        bh[n], bl[n] = split(unpack(msg_b, rc))
    a, b = weights(traces, target)
    old, nb = (ch, cl), (bh, bl)
    for n, (r, s) in enumerate(LOWER):
        p = pc[n] + add_up((lower(old, r, k), upper(nb, k, s)) for k in range(r + 1))
        x = (a * flag(flags, at_c(r, s))) * p + b * xc[n]
        c1[n] = x
        c1h[n], c1l[n] = split(x)
    products = gram((c1h, c1l))
    pack(msg_g, lambda rc: products[rc], [])


def next_rest(
    target, msg_g, xb, xd, xa, pb, pd, pa, c1, flags, old_traces, b1, d1, a1, b1h, b1l, d1h, d1l, a1h, a1l, traces
):
    a, b = weights(old_traces, target)
    t = Traces()
    work = (
        (xa, pa, a1, a1h, a1l, UPPER, at_a),
        (xd, pd, d1, d1h, d1l, LOWER, at_d),
        (xb, pb, b1, b1h, b1l, UPPER, at_b),
    )
    for old, product, new, hi, lo, order, at in work:
        for n, rc in enumerate(order):
            place = at(*rc)
            p = product[n]
            if at is at_b:
                p = p + unpack(msg_g, rc)
            scale = a if place[1] == 0 else a * flag(flags, place)
            x = scale * p + b * old[n]
            new[n] = x
            hi[n], lo[n] = split(x)
            t.add(x, place)
    for n, rc in enumerate(LOWER):
        t.add(c1[n], at_c(*rc))
    t.write(traces)


def across(target, msg_b, msg_g, traces, dep, part, scales):
    del dep
    a, b = weights(traces, target)
    rows = []
    for n, rc in enumerate(UPPER):
        scale = a if rc[0] == rc[1] else a * flag_of(msg_b, rc)
        part[n] = scale * unpack(msg_g, rc) + b * unpack(msg_b, rc)
        rows.append(jnp.broadcast_to(scale, (1, HALF)))
    scales[...] = jnp.concatenate(rows + [jnp.zeros((2, HALF), F32)], axis=0)


def finish_c(target, base, msg_e, part, scales, c1, c1h, c1l, pc1, flags, traces, out, nh, nl, buffer, sems):
    del base
    for n, rc in enumerate(UPPER):
        nh[n], nl[n] = split(part[n] + scales[n : n + 1, 0:1] * unpack(msg_e, rc))
    c, nb = (c1h, c1l), (nh, nl)
    a, b = weights(traces, target)
    copies = []
    for n, (r, s) in enumerate(LOWER):
        place = at_c(r, s)
        p = pc1[n] + add_up((lower(c, r, k), upper(nb, k, s)) for k in range(r + 1))
        buffer[n] = (a * flag(flags, place)) * p + b * c1[n]
        copies.append(pltpu.make_async_copy(buffer.at[n], out.at[place[0], place[1]], sems.at[n]))
        copies[-1].start()
    for copy in copies:
        copy.wait()


def finish_ad(target, pa1, pd1, a1, d1, flags, traces, out, buffer, sems):
    a, b = weights(traces, target)
    copies = []
    groups = ((pd1, d1, LOWER, at_d), (pa1, a1, UPPER, at_a))
    for p, x, order, at in groups:
        for n, rc in enumerate(order):
            place = at(*rc)
            k = len(copies)
            scale = a if place[1] == 0 else a * flag(flags, place)
            buffer[k] = scale * p[n] + b * x[n]
            copies.append(pltpu.make_async_copy(buffer.at[k], out.at[place[0], place[1]], sems.at[k]))
            copies[-1].start()
    for copy in copies:
        copy.wait()


def finish_b(target, base, msg_g, pb1, b1, flags, traces, out, buffer, sems):
    del base
    a, b = weights(traces, target)
    copies = []
    for n, rc in enumerate(UPPER):
        place = at_b(*rc)
        scale = a if place[1] == 0 else a * flag(flags, place)
        buffer[n] = scale * (pb1[n] + unpack(msg_g, rc)) + b * b1[n]
        copies.append(pltpu.make_async_copy(buffer.at[n], out.at[place[0], place[1]], sems.at[n]))
        copies[-1].start()
    for copy in copies:
        copy.wait()


HBM = pl.BlockSpec(memory_space=pltpu.HBM)
ANY = pl.BlockSpec(memory_space=pl.ANY)
VMEM = pl.BlockSpec(memory_space=pltpu.VMEM)
MSG = jax.ShapeDtypeStruct((PACKED, HALF), F32)
SIX = jax.ShapeDtypeStruct((6, BS, BS), F32)
SIX16 = jax.ShapeDtypeStruct((6, BS, BS), BF16)
TRACES = jax.ShapeDtypeStruct((16, HALF), F32)
FLAGS = jax.ShapeDtypeStruct((8, HALF), F32)
PATTERN = [pltpu.SMEM((4, 6), jnp.int32)]
DMA = pltpu.SemaphoreType.DMA


def blocks(n, dtype=F32):
    return pltpu.VMEM((n, BS, BS), dtype)


def call(body, limit, ins, outs, scratch=(), specs=None, out_spec=VMEM, aliases=None, target=None):
    many = isinstance(outs, (list, tuple))
    in_specs = [(specs or {}).get(n, VMEM) for n in range(len(ins))]
    return pl.pallas_call(
        body if target is None else functools.partial(body, target),
        out_shape=outs,
        in_specs=in_specs,
        out_specs=[out_spec] * len(outs) if many else out_spec,
        scratch_shapes=list(scratch),
        input_output_aliases=aliases or {},
        cost_estimate=pl.CostEstimate(flops=1024, bytes_accessed=1024, transcendentals=0),
        compiler_params=pltpu.CompilerParams(vmem_limit_bytes=limit * 2**20),
        name=getattr(body, "__name__", "add_arrays"),
    )(*ins)


def shift(x, step):
    count = lax.axis_size(AXES)
    pairs = [(i, i + step) for i in range(count) if 0 <= i + step < count]
    return lax.ppermute(x, AXES, pairs)


def place_of(i):
    return i // 2 % 4, i // 32, i // 16 % 2 * 2 + i % 2, i // 8 % 2


def index_of(x, y, z, core):
    return ((y % 4 * 2 + z % 4 // 2) * 2 + core % 2) * 8 + x % 4 * 2 + z % 2


def add_arrays(count, *refs):
    total = refs[0][...]
    for ref in refs[1:count]:
        total = total + ref[...]
    refs[-1][...] = total


def total(x, kernels):
    kernels = list(kernels)
    results = []
    count = lax.axis_size(AXES)

    def moved(v, f):
        return lax.ppermute(v, AXES, [(i, f(i)) for i in range(count)])

    def by(f):
        return lambda i: index_of(*f(*place_of(i)))

    def finished(x, arrived):
        ins = [x, *arrived]
        specs = {}
        if kernels:
            results.append(kernels.pop(0)(x))
            last = results[-1]
            specs[len(ins)] = ANY
            ins.append(last[0] if isinstance(last, (list, tuple)) else last)
        return call(functools.partial(add_arrays, 1 + len(arrived)), 1, ins, TRACES, specs=specs)

    if (lax.axis_size("row"), lax.axis_size("col")) != (16, 8):
        for k in range(count.bit_length() - 1):
            x = finished(x, [moved(x, lambda i: i ^ (1 << k))])
    else:
        x = finished(x, [moved(x, by(lambda x, y, z, c: (x, y + k, z + k, c))) for k in (1, 2, 3)])
        x = finished(x, [moved(x, by(lambda x, y, z, c: (x, y + k, z, c))) for k in (1, 2, 3)])
        x = finished(x, [moved(x, by(lambda x, y, z, c: (x, y, z, c + 1)))])

        def ahead(x, z):
            return x + (1 if z % 2 == 0 else -1)

        near = moved(x, by(lambda x, y, z, c: (ahead(x, z), y, z, c)))
        other = moved(x, by(lambda x, y, z, c: (ahead(x, z), y, z // 2 * 2 + 1 - z % 2, c)))
        x = finished(x, [near, other])
        x = finished(x, [moved(near, by(lambda x, y, z, c: (ahead(x, z), y, z, c)))])
    while kernels:
        results.append(kernels.pop(0)(x))
    return x, results


def local(stored, pattern):
    target = float(stored.shape[0] * lax.axis_size(AXES) * stored.shape[2] * 2 // 5)

    pattern = pattern.T
    msg_b, token = call(
        pack_b, 55, (stored, pattern), [MSG, FLAGS], [blocks(6), *PATTERN, DMA((6,)), DMA(())], {0: HBM, 1: HBM}
    )
    next_block = shift(msg_b, -1)
    xc, xa, xd, xb, ch, cl, ah, al, dh, dl, bh, bl, msg_g, traces, flags = call(
        prepare, 40, (stored, pattern, token), [SIX] * 4 + [SIX16] * 8 + [MSG, TRACES, FLAGS],
        [blocks(24), *PATTERN, DMA((24,)), DMA(())], {0: HBM, 1: HBM, 2: ANY},
    )
    from_prev = shift(msg_g, 1)

    traces, (pc, pa, (pb, msg_e), pd) = total(
        traces,
        [
            lambda r: call(product_c, 8, (ah, al, ch, cl, r), SIX, specs={4: ANY}),
            lambda r: call(product_a, 8, (ah, al, ch, cl, dh, dl, r), SIX, specs={6: ANY}),
            lambda r: call(product_b_packed, 8, (bh, bl, dh, dl, r), [SIX, MSG], specs={4: ANY}),
            lambda r: call(product_d, 8, (bh, bl, dh, dl, ah, al, r), SIX, specs={6: ANY}),
        ],
    )

    msg_e, _, _ = lax.optimization_barrier((msg_e, next_block, traces))
    next_e = shift(msg_e, -1)
    c1, c1h, c1l, msg_g1 = call(
        next_c, 14, (next_block, xc, ch, cl, pc, flags, traces), [SIX, SIX16, SIX16, MSG], [blocks(6, BF16)] * 2,
        target=target,
    )
    from_prev1 = shift(msg_g1, 1)
    b1, d1, a1, b1h, b1l, d1h, d1l, a1h, a1l, traces1 = call(
        next_rest, 24, (from_prev, xb, xd, xa, pb, pd, pa, c1, flags, traces), [SIX] * 3 + [SIX16] * 6 + [TRACES],
        target=target,
    )

    traces1, (pa1, pb1, pd1, pc1) = total(
        traces1,
        [
            lambda r: call(product_a, 8, (a1h, a1l, c1h, c1l, d1h, d1l, r), SIX, specs={6: ANY}),
            lambda r: call(product_b, 8, (b1h, b1l, d1h, d1l, r), SIX, specs={4: ANY}),
            lambda r: call(product_d, 8, (b1h, b1l, d1h, d1l, a1h, a1l, r), SIX, specs={6: ANY}),
            lambda r: call(product_c, 8, (a1h, a1l, c1h, c1l, r), SIX, specs={4: ANY}),
        ],
    )
    part, scales = call(
        across, 8, (next_block, msg_g, traces, traces1), [SIX, FLAGS], specs={3: ANY}, target=target
    )
    out = jax.ShapeDtypeStruct(stored.shape, F32)
    done = call(
        finish_ad, 12, (pa1, pd1, a1, d1, flags, traces1), out, [blocks(12), DMA((12,))], None, HBM, target=target
    )
    done = call(
        finish_c, 14, (done, next_e, part, scales, c1, c1h, c1l, pc1, flags, traces1), out,
        [blocks(6, BF16)] * 2 + [blocks(6), DMA((6,))], {0: HBM}, HBM, {0: 0}, target,
    )
    return call(
        finish_b, 8, (done, from_prev1, pb1, b1, flags, traces1), out, [blocks(6), DMA((6,))], {0: HBM}, HBM, {0: 0},
        target,
    )


def solution(mesh):
    in_specs = (P(AXES, None, None, None), P(AXES, None))
    out_specs = P(AXES, None, None, None)
    return jax.shard_map(local, mesh=mesh, in_specs=in_specs, out_specs=out_specs, check_vma=False)
```
